32 devices in a mesh: section: 2 (over core), ctx: 4 (over y, x), exp: 4 (over z).
Axes of the slice: x: 2, y: 2, z: 4, core: 2. Of those that a mesh axis runs over, the one named last changes fastest.
Arguments:
- inputs: bfloat16 [2, 4, 512, 768], P(None, 'exp', 'ctx'), may hold values from -6 to 6
- cotangent: bfloat16 [2, 4, 512, 768], P(None, 'exp', 'ctx'), may hold values from -6 to 6
- segments: int32 [2, 4, 512], P(None, 'exp'), may hold values from 0 to 4, as said below
- buckets: int32 [512], replicated, may hold values from 0 to 63, as said below
- routes: int32 [2, 4, 512, 2], P(None, 'exp', 'ctx'), may hold values from 0 to 7, all different within a row; in each aligned block of 128 rows (0 to 127, 128 to 255, ..., all dimensions but the last counted through in order) at most 40 rows name the same one
- gain_attn: float32 [2, 768], P('section', ('ctx', 'exp')), may hold values from 0.5 to 1.5
- w_query: float32 [2, 768, 768], P('section', ('ctx', 'exp')), may hold values from -0.21875 to 0.21875
- w_key: float32 [2, 768, 768], P('section', ('ctx', 'exp')), may hold values from -0.21875 to 0.21875
- w_value: float32 [2, 768, 768], P('section', ('ctx', 'exp')), may hold values from -0.21875 to 0.21875
- w_out: float32 [2, 768, 768], P('section', ('ctx', 'exp')), may hold values from -0.625 to 0.625
- rel_bias: float32 [2, 64, 12], P('section', ('ctx', 'exp')), may hold values from -4 to 4
- gain_moe: float32 [2, 768], P('section', ('ctx', 'exp')), may hold values from 0.5 to 1.5
- w_router: float32 [2, 768, 8], P('section', ('ctx', 'exp')), may hold values from -0.109375 to 0.109375
- w_in: float32 [2, 8, 768, 3072], P('section', 'exp', 'ctx'), may hold values from -0.21875 to 0.21875
- w_back: float32 [2, 8, 3072, 768], P('section', 'exp', 'ctx'), may hold values from -0.109375 to 0.109375
Outputs:
- activations: float32 [2, 2, 4, 512, 768], P('section', None, 'exp', 'ctx')
- grads_in: float32 [2, 2, 4, 512, 768], P('section', None, 'exp', 'ctx')
- grad_gain_attn: float32 [2, 768], P('section', ('ctx', 'exp'))
- grad_query: float32 [2, 768, 768], P('section', ('ctx', 'exp'))
- grad_key: float32 [2, 768, 768], P('section', ('ctx', 'exp'))
- grad_value: float32 [2, 768, 768], P('section', ('ctx', 'exp'))
- grad_outproj: float32 [2, 768, 768], P('section', ('ctx', 'exp'))
- grad_rel_bias: float32 [2, 64, 12], P('section', ('ctx', 'exp'))
- grad_gain_moe: float32 [2, 768], P('section', ('ctx', 'exp'))
- grad_router: float32 [2, 768, 8], P('section', ('ctx', 'exp'))
- grad_w_in: float32 [2, 8, 768, 3072], P('section', 'exp', 'ctx')
- grad_w_back: float32 [2, 8, 3072, 768], P('section', 'exp', 'ctx')
The draws below stay inside these ranges and needn't reach their ends.
Inputs may be any that keep to these rules, and one draw needn't show every extreme that they name: `segments`: each sequence is a prompt (segment 0) of 128 to 448 positions followed by 4 continuations of near-equal length in increasing order; the last position is in segment 4; in each micro-batch one sequence has a prompt of exactly 448 positions. `buckets`: never falling in the distance; 0 at distance 0 and 63 at the largest distance. `routes`: each position names two different experts; among the 128 positions of one device in one micro-batch, at most 40 name the same expert, a bound that some block reaches.
All inputs are finite; a program needn't handle non-finite values.
Results may differ from the reference program's by a relative error of at most 0.035.
Values may be sent and summed in bfloat16 or wider, within the bound.
No kernel may reach another device: no remote copies, remote signals or barrier semaphores. Data moves between devices by JAX's collectives and lax.ppermute only.
A program may use at most 320 MiB of HBM per device.

```python
import math
import jax
import jax.numpy as jnp
import numpy as np
from jax import lax

D = 768
HEADS = 12
HEAD_DIM = 64
FF = 3072
TOK_DEV = 128
MICRO = 2
CONT = 4
NB = 64
EXPERTS = 8
SEQ = 512
SEQS = 4
CAP = 40
N_CTX = 4


def draw_segments(key, part):
    key = jax.random.fold_in(key, 11)
    key_prompt, key_whole = jax.random.split(key)
    prompt = jax.random.randint(key_prompt, (MICRO, SEQS, 1), SEQ // 4, SEQ // 2 + 1).astype(jnp.int32)
    whole_seq = jax.random.randint(key_whole, (MICRO, 1, 1), 0, SEQS).astype(jnp.int32)
    seq_ids = jnp.arange(SEQS, dtype=jnp.int32)[None, :, None]
    prompt = jnp.where(seq_ids == whole_seq, SEQ - SEQ // 8, prompt).astype(jnp.int32)
    position = jnp.arange(SEQ, dtype=jnp.int32)[None, None, :]
    after_prompt = jnp.maximum(position - prompt, 0)
    labels = jnp.where(position < prompt, 0, 1 + after_prompt * CONT // (SEQ - prompt))
    return labels.astype(jnp.int32)


def draw_buckets(key, part):
    key = jax.random.fold_in(key, 23)
    shuffled = jax.random.permutation(key, SEQ - 1) + 1
    bounds = jnp.sort(shuffled[:NB - 1])
    distance = jnp.arange(SEQ, dtype=jnp.int32)
    return jnp.sum((distance[:, None] >= bounds[None, :]).astype(jnp.int32), axis=1).astype(jnp.int32)


def block_levels(own_key, shape, shards, smallest, high):
    def one(axis_at, shards_of):
        steps = jax.random.uniform(jax.random.fold_in(jax.random.fold_in(own_key, 6), axis_at), (shards_of,), jnp.float32, smallest / len(shards), high / len(shards))
        return jnp.repeat(jnp.exp(steps), shape[axis_at] // shards_of).reshape((-1,) + (1,) * (len(shape) - axis_at - 1))

    gain = one(*shards[0])
    for cut in shards[1:]:
        gain = gain * one(*cut)
    return gain


def routed_block(stream_key, own, number, rows, number_of, top, reach, lean):
    order = jax.random.permutation(stream_key, number_of)
    packed, ordinary = load_shares(number_of, rows * top, reach, lean, True), load_shares(number_of, rows * top, reach, lean, False)
    places = jnp.arange(number_of)

    def named(lengths, turn):
        used = int((lengths > 0).sum())
        fixed = max(1, used // 4)
        shifted = fixed + (places - fixed + turn * (used - fixed)) % max(1, number_of - fixed)
        return jnp.zeros((number_of,), jnp.int32).at[order[jnp.where(places < fixed, places, shifted)]].set(jnp.asarray(lengths, jnp.int32))

    lengths = jnp.where(number % 4 == 0, named(packed, number // 4), named(ordinary, number - number // 4 - 1))
    mixed = jax.random.permutation(jax.random.fold_in(own, 3), number_of)
    giver, receiver = mixed[0:number_of // 2 * 2:2], mixed[1:number_of // 2 * 2:2]
    slack = jnp.minimum(lengths[giver] - 1, reach - lengths[receiver]) // 2
    slack = jnp.where((giver == order[0]) | (receiver == order[0]) | (lengths[receiver] == 0), 0, jnp.maximum(slack, 0))
    shifted = jax.random.randint(jax.random.fold_in(own, 4), (number_of // 2,), 0, 1 << 20) % (slack + 1)
    lengths = lengths.at[giver].add(-shifted).at[receiver].add(shifted)
    members = jnp.searchsorted(jnp.cumsum(lengths), jnp.arange(rows * top), side="right").astype(jnp.int32)
    table = members.reshape(top, rows).T
    table = table[jax.random.permutation(jax.random.fold_in(own, 1), rows)]
    turn = jax.random.randint(jax.random.fold_in(own, 2), (rows, 1), 0, top)
    return jnp.take_along_axis(table, (jnp.arange(top)[None, :] + turn) % top, axis=1)


def load_shares(amount, total, limit, lean, full):
    weights = [(1 << 20) // math.isqrt(standing ** lean) + 1 for standing in range(1, amount + 1)]
    largest = limit if full else min(limit, max(-(-total // amount), total * weights[0] // sum(weights)))
    least = 1 if total - largest >= amount - 1 else 0
    given, rest = [largest] + [least] * (amount - 1), total - largest - least * (amount - 1)
    while rest > 0:
        candidates = [i for i in range(1, amount) if given[i] < largest] or [i for i in range(1, amount) if given[i] < limit]
        pool, remaining = sum([weights[i] for i in candidates]), rest
        for i in candidates:
            extra = min(limit - given[i], max(1, remaining * weights[i] // pool), rest)
            given[i] = given[i] + extra
            rest = rest - extra
    return np.array(given)


def gaussian(stream_key, dims, scale, limit, cuts=(), kind=jnp.bfloat16):
    loudness = block_levels(stream_key, dims, cuts, -0.22, 0.18) if cuts else 1.0
    array = jax.random.normal(stream_key, dims, jnp.float32) * scale * loudness
    return jnp.minimum(jnp.maximum(array, -limit), limit).astype(kind)


def setup_inputs(seed: int = 0) -> dict:
    key_of = jax.random.split(jax.random.key(seed), 16)
    inputs = gaussian(key_of[0], (MICRO, SEQS, SEQ, D), 1.0, 6.0, ((1, 4), (2, 4)))
    cotangent = gaussian(key_of[1], (MICRO, SEQS, SEQ, D), 1.0, 6.0, ((1, 4), (2, 4)))
    segments = draw_segments(jax.random.fold_in(key_of[15], 71), 0)
    buckets = draw_buckets(jax.random.fold_in(key_of[15], 71), 0)
    routes_keys = jax.random.split(jax.random.fold_in(key_of[4], 1), MICRO * SEQS * SEQ // TOK_DEV)
    routes_turns = jax.random.permutation(jax.random.fold_in(key_of[4], 3), MICRO * SEQS * SEQ // TOK_DEV)
    routes = jax.vmap(lambda own, number: routed_block(jax.random.fold_in(key_of[4], 2), own, number, TOK_DEV, EXPERTS, 2, CAP, 1))(routes_keys, routes_turns).reshape((MICRO, SEQS, SEQ, 2))
    gain_attn = jnp.clip(1.0 + 0.1 * jax.random.normal(key_of[5], (2, D), jnp.float32), 0.5, 1.5)
    w_query = gaussian(key_of[6], (2, D, D), D ** -0.5, 0.21875, ((0, 2), (1, 16)), jnp.float32)
    w_key = gaussian(key_of[7], (2, D, D), D ** -0.5, 0.21875, ((0, 2), (1, 16)), jnp.float32)
    w_value = gaussian(key_of[8], (2, D, D), D ** -0.5, 0.21875, ((0, 2), (1, 16)), jnp.float32)
    w_out = gaussian(key_of[9], (2, D, D), (D // 8) ** -0.5, 0.625, ((0, 2), (1, 16)), jnp.float32)
    rel_bias = gaussian(key_of[10], (2, NB, HEADS), 1.0, 4.0, ((0, 2), (1, 16)), jnp.float32)
    gain_moe = jnp.clip(1.0 + 0.1 * jax.random.normal(key_of[11], (2, D), jnp.float32), 0.5, 1.5)
    w_router = gaussian(key_of[12], (2, D, EXPERTS), (4 * D) ** -0.5, 0.109375, ((0, 2), (1, 16)), jnp.float32)
    w_in = gaussian(key_of[13], (2, EXPERTS, D, FF), D ** -0.5, 0.21875, ((0, 2), (1, 4), (2, 4)), jnp.float32)
    w_back = gaussian(key_of[14], (2, EXPERTS, FF, D), FF ** -0.5, 0.109375, ((0, 2), (1, 4), (2, 4)), jnp.float32)
    return {"inputs": inputs, "cotangent": cotangent, "segments": segments, "buckets": buckets, "routes": routes, "gain_attn": gain_attn, "w_query": w_query, "w_key": w_key, "w_value": w_value, "w_out": w_out, "rel_bias": rel_bias, "gain_moe": gain_moe, "w_router": w_router, "w_in": w_in, "w_back": w_back}


@jax.custom_vjp
def low(v):
    return lax.optimization_barrier(v.astype(jnp.bfloat16)).astype(jnp.float32)

@jax.custom_vjp
def low_back(v):
    return v

def low_keep(v):
    return (low(v), None)

def low_pass(kept, grad):
    return (grad,)

def back_keep(v):
    return (v, None)

def back_low(kept, grad):
    return (low(grad),)
low.defvjp(low_keep, low_pass)
low_back.defvjp(back_keep, back_low)
EPS = 1e-06
HIGH = lax.Precision.HIGHEST

def rms_norm(value, gain_row):
    return value * lax.rsqrt(lax.optimization_barrier(jnp.mean(value * value, axis=-1, keepdims=True)) + EPS) * gain_row

def attend_sequence(queries, keys_all, values_all, seg_row, buckets, rel_table):
    block_rows = min(512, SEQ)
    score_scale = HEAD_DIM ** (-0.5)
    key_pos = jnp.arange(SEQ, dtype=jnp.int32)

    def one_block(row_start):
        query_part = lax.dynamic_slice_in_dim(queries, row_start, block_rows, 0)
        query_seg = lax.dynamic_slice_in_dim(seg_row, row_start, block_rows, 0)
        query_pos = row_start + jnp.arange(block_rows, dtype=jnp.int32)
        distance = query_pos[:, None] - key_pos[None, :]
        allowed = (distance >= 0) & ((seg_row[None, :] == 0) | (seg_row[None, :] == query_seg[:, None]))
        bucket_index = jnp.take(buckets, jnp.clip(distance, 0, SEQ - 1))
        bias_grid = jnp.transpose(jnp.take(rel_table, bucket_index, axis=0), (2, 0, 1))
        scores = jnp.einsum('qhd,khd->hqk', query_part, keys_all, precision=HIGH) * score_scale + bias_grid
        scores = low_back(scores)
        scores = jnp.where(allowed[None], scores, -1e+30)
        probs = jax.nn.softmax(scores, axis=-1)
        return jnp.einsum('hqk,khd->qhd', low(probs), values_all, precision=HIGH)
    starts = jnp.arange(SEQ // block_rows, dtype=jnp.int32) * block_rows
    result = lax.map(jax.checkpoint(one_block), starts)
    return result.reshape(SEQ, HEADS, HEAD_DIM)

def layer(layer_input, segments, buckets, routes, params):
    gain_early, query_w, key_w, value_w, outproj_w, bias_table, gain_late, router_w, w_first, w_second = params
    normed_attn = low(rms_norm(layer_input, low(gain_early)))

    def project(weight):
        return low(low_back(jnp.einsum('mbld,de->mble', normed_attn, low(weight), precision=HIGH)))
    queries = project(query_w)
    keys_all = project(key_w)
    values_all = project(value_w)
    seq_count = MICRO * SEQS
    shape_four = (seq_count, SEQ, HEADS, HEAD_DIM)
    table_low = low(bias_table)

    def per_sequence(seq_items):
        query_seq, key_seq, value_seq, segment_seq = seq_items
        return attend_sequence(query_seq, key_seq, value_seq, segment_seq, buckets, table_low)
    attended = lax.map(per_sequence, (queries.reshape(shape_four), keys_all.reshape(shape_four), values_all.reshape(shape_four), segments.reshape(seq_count, SEQ)))
    attended = low(low_back(attended.reshape(MICRO, SEQS, SEQ, D)))
    residual = layer_input + low_back(jnp.einsum('mbld,de->mble', attended, low(outproj_w), precision=HIGH))
    normed_moe = low(rms_norm(residual, low(gain_late)))
    logits = low_back(jnp.einsum('mbld,de->mble', normed_moe, low(router_w), precision=HIGH))
    chosen = jnp.take_along_axis(logits, routes, axis=-1)
    gate_probs = jax.nn.softmax(chosen, axis=-1)
    blocks = MICRO * SEQS * N_CTX
    flat_routes = routes.reshape(blocks, 2 * TOK_DEV)
    member = (flat_routes[..., None] == jnp.arange(EXPERTS, dtype=jnp.int32)).astype(jnp.int32)
    slot_rank = lax.optimization_barrier(jnp.sum((jnp.cumsum(member, axis=1) - member) * member, axis=-1))
    slot_dest = (flat_routes * CAP + slot_rank).astype(jnp.int32)
    token_rows = normed_moe.reshape(blocks, TOK_DEV, D)
    source = jnp.arange(2 * TOK_DEV, dtype=jnp.int32) // 2

    def fill_block(rows_block, dest_block):
        return jnp.zeros((EXPERTS * CAP, D), jnp.float32).at[dest_block].set(rows_block[source])
    buffers = low_back(jax.vmap(fill_block)(token_rows, slot_dest))
    by_expert = buffers.reshape(blocks, EXPERTS, CAP, D).transpose(1, 0, 2, 3).reshape(EXPERTS, blocks * CAP, D)

    def expert_apply(expert_items):
        rows_in, first_w, second_w = expert_items
        hidden_pre = low_back(jnp.dot(rows_in, first_w, precision=HIGH, preferred_element_type=jnp.float32))
        activated = low(jax.nn.gelu(hidden_pre))
        return low(low_back(jnp.dot(activated, second_w, precision=HIGH, preferred_element_type=jnp.float32)))
    results = lax.map(jax.checkpoint(expert_apply), (by_expert, low(w_first), low(w_second)))
    results = results.reshape(EXPERTS, blocks, CAP, D).transpose(1, 0, 2, 3).reshape(blocks, EXPERTS * CAP, D)

    def take_rows(res_block, dest_block):
        return res_block[dest_block]
    picked = jax.vmap(take_rows)(results, slot_dest).reshape(MICRO, SEQS, SEQ, 2, D)
    return residual + lax.optimization_barrier(jnp.sum(gate_probs[..., None] * picked, axis=-2))

def reference(inputs, cotangent, segments, buckets, routes, gain_attn, w_query, w_key, w_value, w_out, rel_bias, gain_moe, w_router, w_in, w_back):
    params = (gain_attn.astype(jnp.float32), w_query.astype(jnp.float32), w_key.astype(jnp.float32), w_value.astype(jnp.float32), w_out.astype(jnp.float32), rel_bias.astype(jnp.float32), gain_moe.astype(jnp.float32), w_router.astype(jnp.float32), w_in.astype(jnp.float32), w_back.astype(jnp.float32))
    input_float = inputs.astype(jnp.float32)
    shift_zero = jnp.zeros_like(input_float)

    def two_sections(input_value, shift_value, *weights):
        section_one = layer(input_value, segments, buckets, routes, tuple((weight[0] for weight in weights)))
        passed = low(low_back(section_one)) + shift_value
        section_two = layer(passed, segments, buckets, routes, tuple((weight[1] for weight in weights)))
        return (section_two, section_one)
    section_two, back_fn, section_one = jax.vjp(two_sections, input_float, shift_zero, *params, has_aux=True)
    all_grads = back_fn(cotangent.astype(jnp.float32))
    activations = jnp.stack([section_one, section_two])
    grads_in = jnp.stack([all_grads[0], all_grads[1]])
    return (activations, grads_in, all_grads[2], all_grads[3], all_grads[4], all_grads[5], all_grads[6], all_grads[7], all_grads[8], all_grads[9], all_grads[10], all_grads[11])
```

```python
import functools

import jax
import jax.numpy as jnp
from jax import lax
from jax.experimental import pallas as pl
from jax.experimental.pallas import tpu as pltpu
from jax.sharding import PartitionSpec as P

EPS = 1e-06
NEG = -1e30
LOW = jnp.bfloat16
WIDE = jnp.float32
VMEM_BYTES = 48 * 1024 * 1024


def swapped(block):
    return lax.ppermute(block, "section", [(0, 1), (1, 0)])


def shifted(block, distance):
    size = lax.axis_size("ctx")
    route = [(i, i + distance) for i in range(size) if 0 <= i + distance < size]
    return lax.ppermute(block, "ctx", route)


def crossed(block, bits, axis="ctx"):
    return lax.ppermute(block, axis, [(i, i ^ bits) for i in range(lax.axis_size(axis))])


def tied(value, *others):
    return lax.optimization_barrier((value, *others))[0]


def place_kernel(moves, count, rank_ref, *refs):
    out_ref, sems = refs[count:]
    copies = []
    for number, (at, first, size, fixed, relation) in enumerate(moves):
        start = fixed + (rank_ref[0] ^ relation) * size
        target = out_ref.at[pl.ds(pl.multiple_of(start, 16), size)]
        copies.append(
            pltpu.make_async_copy(refs[at].at[pl.ds(first, size)], target, sems.at[number])
        )
        copies[-1].start()
    for one in copies:
        one.wait()


def placed(rank, pieces, moves, rows):
    return pl.pallas_call(
        functools.partial(place_kernel, moves, len(pieces)),
        out_shape=jax.ShapeDtypeStruct((rows, pieces[0].shape[1]), pieces[0].dtype),
        in_specs=[
            pl.BlockSpec(memory_space=pltpu.SMEM),
            *[pl.BlockSpec(memory_space=pl.ANY)] * len(pieces),
        ],
        out_specs=in_vmem(1)[0],
        scratch_shapes=[pltpu.SemaphoreType.DMA((len(moves),))],
        compiler_params=pltpu.CompilerParams(vmem_limit_bytes=VMEM_BYTES),
    )(rank.reshape(1), *pieces)


def four_by_four():
    return lax.axis_size("ctx") == 4 and lax.axis_size("exp") == 4


def exp_line(block):
    if not four_by_four():
        return [block] * 2, lax.all_gather(block, "exp", axis=0, tiled=True)
    shard = block.shape[0]
    along_exp = [block] + [crossed(block, k, "exp") for k in (1, 2, 3)]
    moves = [(k, 0, shard, 0, k) for k in range(4)]
    return along_exp, placed(lax.axis_index("exp"), along_exp, moves, 4 * shard)


def ctx_rows(line, before_relay):
    if not four_by_four():
        return lax.all_gather(line, "ctx", axis=0, tiled=True)
    from_x, from_y = crossed(line, 1), crossed(line, 2)
    along_ctx = [line, from_x, from_y, crossed(tied(from_x, *before_relay), 2)]
    size = line.shape[0]
    moves = [(k, 0, size, 0, k) for k in range(4)]
    return placed(lax.axis_index("ctx"), along_ctx, moves, 4 * size)


def plane_rows(block):
    from_x, from_y = crossed(block, 1), crossed(block, 2)
    along_ctx = [block, from_x, from_y, crossed(from_x, 2)]
    shard = block.shape[0]
    moves = [(k, 0, shard, 0, k) for k in range(4)]
    return placed(lax.axis_index("ctx"), along_ctx, moves, 4 * shard)


def all_rows(planes, shard):
    moves = [(k, at * shard, shard, at * 4 * shard, k) for k in range(4) for at in range(4)]
    return placed(lax.axis_index("exp"), planes, moves, 16 * shard)


def added(left, right):
    return left.astype(WIDE) + right.astype(WIDE)


def first_hop(parts, near, far):
    relayed = added(parts[far], crossed(parts[3], near)).astype(LOW)
    return added(parts[0], crossed(parts[near], near)), relayed


def last_hop(state, far):
    mine, relayed = state
    return mine + crossed(relayed, far).astype(WIDE)


def parts_for(blocks, axis, name):
    rank = lax.axis_index(name)
    return [lax.dynamic_index_in_dim(blocks, rank ^ k, axis, keepdims=False) for k in range(4)]


def over_exp(parts, came):
    total = parts[0].astype(WIDE)
    for one in came:
        total = total + one.astype(WIDE)
    return total


def over_ctx(parts):
    return last_hop(first_hop(parts, 2, 1), 1)


def sent_along_exp(parts):
    return [crossed(parts[k], k, "exp") for k in (1, 2, 3)]


def finished_along_ctx(parts, came):
    return over_ctx(parts_for(over_exp(parts, came).astype(LOW), 0, "ctx"))


def finished_along_exp(part):
    shard = part.shape[0] // 4
    parts = parts_for(part.astype(LOW).reshape(4, shard, part.shape[1]), 0, "exp")
    return over_exp(parts, sent_along_exp(parts))


def scattered_rows(block):
    block = lax.psum_scatter(block, "ctx", scatter_dimension=0, tiled=True)
    return lax.psum_scatter(block, "exp", scatter_dimension=0, tiled=True).astype(WIDE)


def dense_grads_kernel(ranks, normed_ref, grad_ref, attn_ref, branch_ref, small_ref, *refs):
    early_outs, late_outs, early, late = refs[:4], refs[4:8], refs[8], refs[9]
    cut, half = early.shape[1], branch_ref.shape[1]
    rest = grad_ref.shape[1] - cut
    early[...] = dot_dims(normed_ref[...], grad_ref[:, :cut], 0, 0).astype(LOW)
    late[:, :rest] = dot_dims(normed_ref[...], grad_ref[:, cut:], 0, 0).astype(LOW)
    late[:, rest : rest + half] = dot_dims(attn_ref[...], branch_ref[...], 0, 0).astype(LOW)
    late[:, rest + half :] = small_ref[...]
    shard = early.shape[0] // 16

    def rows_at(start):
        return pl.ds(pl.multiple_of(start, 16), shard)

    for k in range(4):
        at_exp = (ranks[1] ^ k) * shard
        for at in range(4):
            late_outs[k][at] = late[rows_at(at * 4 * shard + at_exp), :]
            start = (ranks[0] ^ k) * 4 * shard + at * shard
            early_outs[k][at * shard : (at + 1) * shard] = early[rows_at(start), :]


def dense_grads(normed_a, grad_qkv, attn_low, branch, small):
    width, half = normed_a.shape[1], branch.shape[1]
    shard = width // 16
    late_columns = half + half + small.shape[1]
    shapes = [(4 * shard, 2 * half)] * 4 + [(4, shard, late_columns)] * 4
    ranks = jnp.stack([lax.axis_index("ctx"), lax.axis_index("exp")]).astype(jnp.int32)
    out = pl.pallas_call(
        dense_grads_kernel,
        out_shape=[jax.ShapeDtypeStruct(one, LOW) for one in shapes],
        in_specs=[pl.BlockSpec(memory_space=pltpu.SMEM), *in_vmem(5)],
        out_specs=in_vmem(8),
        scratch_shapes=[pltpu.VMEM((width, 2 * half), LOW), pltpu.VMEM((width, late_columns), LOW)],
        compiler_params=pltpu.CompilerParams(vmem_limit_bytes=VMEM_BYTES),
    )(ranks, normed_a, grad_qkv, attn_low, branch, small)
    return out[:4], out[4:]


def in_vmem(count):
    return [pl.BlockSpec(memory_space=pltpu.VMEM)] * count


def dot_wide(left, right):
    return jnp.dot(left, right, preferred_element_type=WIDE)


def dot_dims(left, right, left_dim, right_dim):
    return lax.dot_general(
        left, right, (((left_dim,), (right_dim,)), ((), ())), preferred_element_type=WIDE
    )


def bias_kernel(rows, blocks, vec_ref, out_ref):
    for head in range(vec_ref.shape[0]):
        for at in range(blocks):
            wide = jnp.broadcast_to(vec_ref[head, at], (rows, 2 * rows))
            turned = pltpu.roll(wide, rows + 1, 1, stride=1, stride_axis=0)
            out_ref[
                head // 2, pl.ds((head % 2) * rows, rows), pl.ds(at * rows, rows)
            ] = turned[:, :rows]


def bias_blocks(vec, rows, blocks):
    heads = vec.shape[0]
    return pl.pallas_call(
        functools.partial(bias_kernel, rows, blocks),
        out_shape=jax.ShapeDtypeStruct((heads // 2, 2 * rows, blocks * rows), WIDE),
        in_specs=in_vmem(1),
        out_specs=in_vmem(1)[0],
        compiler_params=pltpu.CompilerParams(vmem_limit_bytes=VMEM_BYTES),
    )(vec)


def mask_rows(rows, at_q, key_blocks, seg_q, segk_ref):
    parts = []
    for back, at_k in enumerate(key_blocks):
        seg_k = segk_ref[at_k]
        good = (seg_k == 0) | (seg_k == seg_q)
        if back == 0:
            q_at = lax.broadcasted_iota(jnp.int32, (rows, rows), 0)
            k_at = lax.broadcasted_iota(jnp.int32, (rows, rows), 1)
            good = good & (q_at >= k_at)
        parts.append(jnp.where(good, 0.0, NEG).astype(WIDE))
    one = jnp.concatenate(parts, axis=1)
    return jnp.concatenate([one, one], axis=0)


def stacked_pair(block, half):
    lane = lax.broadcasted_iota(jnp.int32, block.shape, 1)
    zero = jnp.zeros_like(block)
    return jnp.concatenate(
        [jnp.where(lane < half, block, zero), jnp.where(lane >= half, block, zero)], axis=0
    )


def unstacked_pair(block, half):
    rows = block.shape[0] // 2
    lane = lax.broadcasted_iota(jnp.int32, (rows, block.shape[1]), 1)
    return jnp.where(lane < half, block[:rows], block[rows:])


def key_order(at_q, held, groups):
    near = [(0, at) for at in range(at_q, -1, -1)]
    return near + [(group, at) for group in range(1, groups) for at in range(held - 1, -1, -1)]


def attend_kernel(held, rows, groups, head_dim, *refs):
    q_ref, kv_refs = refs[0], refs[1 : 1 + groups]
    bias_ref, segq_ref, segk_ref, wide_ref, low_ref, log_ref = refs[1 + groups :]
    pairs = bias_ref.shape[0]
    lanes = 2 * head_dim
    width = pairs * lanes
    for at_q in range(held):
        order = key_order(at_q, held, groups)
        mask = mask_rows(rows, at_q, [g * held + at for g, at in order], segq_ref[at_q], segk_ref)
        here = pl.ds(at_q * rows, rows)
        for pair in range(pairs):
            cols = pl.ds(pair * lanes, lanes)
            vcols = pl.ds(width + pair * lanes, lanes)
            query = stacked_pair(q_ref[here, cols] * (head_dim**-0.5), head_dim)
            keys = jnp.concatenate(
                [kv_refs[g][pl.ds(at * rows, rows), cols] for g, at in order], axis=0
            )
            values = jnp.concatenate(
                [kv_refs[g][pl.ds(at * rows, rows), vcols] for g, at in order], axis=0
            )
            bias = bias_ref[pair, :, pl.ds(0, len(order) * rows)]
            scores = dot_dims(query, keys, 1, 1) + bias + mask
            top = jnp.max(scores, axis=1, keepdims=True)
            weights = jnp.exp(scores - top)
            total = jnp.sum(weights, axis=1, keepdims=True)
            out = dot_wide(weights.astype(LOW), values) / total
            log_ref[at_q * pairs + pair] = top + jnp.log(total)
            out = unstacked_pair(out, head_dim)
            wide_ref[here, cols] = out
            low_ref[here, cols] = out.astype(LOW)


def attend(query, kv_groups, bias, seg_q, seg_k, rows, head_dim):
    groups = len(kv_groups)
    held = query.shape[0] // rows
    pairs = bias.shape[0]
    return pl.pallas_call(
        functools.partial(attend_kernel, held, rows, groups, head_dim),
        out_shape=(
            jax.ShapeDtypeStruct(query.shape, WIDE),
            jax.ShapeDtypeStruct(query.shape, LOW),
            jax.ShapeDtypeStruct((held * pairs, 2 * rows, 1), WIDE),
        ),
        in_specs=in_vmem(4 + groups),
        out_specs=tuple(in_vmem(3)),
        compiler_params=pltpu.CompilerParams(vmem_limit_bytes=VMEM_BYTES),
    )(query, *kv_groups, bias, seg_q, seg_k)


def diagonal_sums(block):
    rows = block.shape[0]
    wide = jnp.concatenate([block, jnp.zeros_like(block)], axis=1)
    while rows > 8:
        rows //= 2
        wide = pltpu.roll(wide[:rows], rows, 1) + wide[rows:]
    row_at = lax.broadcasted_iota(jnp.int32, wide.shape, 0)
    for step in (4, 2, 1):
        wide = jnp.where(((7 - row_at) & step) != 0, pltpu.roll(wide, step, 1), wide)
    return jnp.sum(wide, axis=0, keepdims=True)


def attend_back_kernel(held, rows, groups, head_dim, *refs):
    q_ref, kv_refs = refs[0], refs[1 : 1 + groups]
    bias_ref, segq_ref, segk_ref, log_ref, grad_ref, wide_ref = refs[1 + groups : 7 + groups]
    dq_ref, dkv_refs = refs[7 + groups], refs[8 + groups : 8 + 2 * groups]
    diag_ref, acc_ref, dkv_acc = refs[8 + 2 * groups :]
    pairs = bias_ref.shape[0]
    lanes = 2 * head_dim
    width = pairs * lanes
    scale = head_dim**-0.5
    seen = set()

    def add_to(group, at, cols, block):
        here = pl.ds(at * rows, rows)
        if (group, at, cols.start) in seen:
            dkv_acc[group, here, cols] += block
        else:
            seen.add((group, at, cols.start))
            dkv_acc[group, here, cols] = block

    for at_q in range(held - 1, -1, -1):
        order = key_order(at_q, held, groups)
        mask = mask_rows(rows, at_q, [g * held + at for g, at in order], segq_ref[at_q], segk_ref)
        here = pl.ds(at_q * rows, rows)
        for pair in range(pairs):
            cols = pl.ds(pair * lanes, lanes)
            vcols = pl.ds(width + pair * lanes, lanes)
            query = stacked_pair(q_ref[here, cols] * scale, head_dim)
            grad = stacked_pair(grad_ref[here, cols], head_dim)
            wide = stacked_pair(wide_ref[here, cols], head_dim)
            delta = jnp.sum(grad.astype(WIDE) * wide, axis=1, keepdims=True)
            keys = jnp.concatenate(
                [kv_refs[g][pl.ds(at * rows, rows), cols] for g, at in order], axis=0
            )
            values = jnp.concatenate(
                [kv_refs[g][pl.ds(at * rows, rows), vcols] for g, at in order], axis=0
            )
            span = pl.ds(0, len(order) * rows)
            scores = dot_dims(query, keys, 1, 1) + bias_ref[pair, :, span] + mask
            probs = jnp.exp(scores - log_ref[at_q * pairs + pair])
            grad_probs = dot_dims(grad, values, 1, 1)
            grad_scores = (probs * (grad_probs - delta)).astype(LOW)
            grad_query = unstacked_pair(dot_wide(grad_scores, keys) * scale, head_dim)
            dq_ref[here, cols] = grad_query.astype(LOW)
            grad_keys = dot_dims(grad_scores, query, 0, 0)
            grad_values = dot_dims(probs.astype(LOW), grad, 0, 0)
            for back, (group, at) in enumerate(order):
                part = slice(back * rows, (back + 1) * rows)
                add_to(group, at, cols, grad_keys[part])
                add_to(group, at, vcols, grad_values[part])
            if at_q == held - 1:
                acc_ref[pair] = grad_scores.astype(WIDE)
            else:
                acc_ref[pair, :, span] += grad_scores.astype(WIDE)
    for group in range(groups):
        dkv_refs[group][...] = dkv_acc[group].astype(dkv_refs[group].dtype)
    for pair in range(pairs):
        for head in range(2):
            for at in range(held * groups):
                block = acc_ref[pair, pl.ds(head * rows, rows), pl.ds(at * rows, rows)]
                diag_ref[2 * pair + head, at] = diagonal_sums(block)


def attend_back(query, kv_groups, bias, seg_q, seg_k, log_total, grad, wide, rows, head_dim):
    groups = len(kv_groups)
    held = query.shape[0] // rows
    pairs = bias.shape[0]
    kv_shape = kv_groups[0].shape
    return pl.pallas_call(
        functools.partial(attend_back_kernel, held, rows, groups, head_dim),
        out_shape=(
            jax.ShapeDtypeStruct(query.shape, LOW),
            jax.ShapeDtypeStruct(kv_shape, WIDE),
            *[jax.ShapeDtypeStruct(kv_shape, LOW)] * (groups - 1),
            jax.ShapeDtypeStruct((2 * pairs, held * groups, 1, 2 * rows), WIDE),
        ),
        in_specs=in_vmem(7 + groups),
        out_specs=tuple(in_vmem(2 + groups)),
        scratch_shapes=[pltpu.VMEM(bias.shape, WIDE), pltpu.VMEM((groups, *kv_shape), WIDE)],
        compiler_params=pltpu.CompilerParams(vmem_limit_bytes=VMEM_BYTES),
    )(query, *kv_groups, bias, seg_q, seg_k, log_total, grad, wide)


GELU_A = 0.7978845608028654
GELU_B = 0.044715


def gelu_of(pre):
    return 0.5 * pre * (1.0 + jnp.tanh(GELU_A * (pre + GELU_B * pre * pre * pre)))


def gelu_and_slope(pre):
    square = pre * pre
    bent = jnp.tanh(GELU_A * pre * (1.0 + GELU_B * square))
    half_up = 0.5 * (1.0 + bent)
    slope = half_up + 0.5 * pre * (1.0 - bent * bent) * (
        GELU_A * (1.0 + 3.0 * GELU_B * square)
    )
    return pre * half_up, slope


def any_specs(count):
    return [pl.BlockSpec(memory_space=pl.ANY)] * count


CHUNKS = 4


class Chunks:
    def __init__(self, first_hbm, second_hbm, first, second, sems):
        hidden = second.shape[1]
        self.first_copies = [
            pltpu.make_async_copy(
                first_hbm.at[:, at * hidden : (at + 1) * hidden], first.at[at], sems.at[0, at]
            )
            for at in range(CHUNKS)
        ]
        self.second_copies = [
            pltpu.make_async_copy(
                second_hbm.at[at * hidden : (at + 1) * hidden], second.at[at], sems.at[1, at]
            )
            for at in range(CHUNKS)
        ]
        for first_copy, second_copy in zip(self.first_copies, self.second_copies):
            first_copy.start()
            second_copy.start()


def experts_forward_steps(chunks, x, first, second, total, pre_ref):
    for at in range(CHUNKS):
        chunks.first_copies[at].wait()
        pre = dot_wide(x, first[at])
        pre_ref[at] = pre
        act = gelu_of(pre).astype(LOW)
        chunks.second_copies[at].wait()
        part = dot_wide(act, second[at])
        total[...] = part if at == 0 else total[...] + part


def experts_back_steps(x, grad, pre_ref, first, second, total, gfirst, gsecond, outs, sems, chunks):
    out_first, out_second = outs
    hidden = second.shape[1]
    copies = []
    for at in range(CHUNKS):
        if chunks is not None:
            chunks.second_copies[at].wait()
            chunks.first_copies[at].wait()
        here = slice(at * hidden, (at + 1) * hidden)
        act, slope = gelu_and_slope(pre_ref[at])
        if gsecond is not None:
            gsecond[at] = dot_dims(act.astype(LOW), grad, 0, 0).astype(LOW)
            copies.append(
                pltpu.make_async_copy(gsecond.at[at], out_second.at[here], sems.at[1, at])
            )
            copies[-1].start()
        grad_act = dot_dims(grad, second[at], 1, 1)
        grad_pre = (grad_act * slope).astype(LOW)
        gfirst[at] = dot_dims(x, grad_pre, 0, 0).astype(LOW)
        copies.append(pltpu.make_async_copy(gfirst.at[at], out_first.at[:, here], sems.at[0, at]))
        copies[-1].start()
        part = dot_dims(grad_pre, first[at], 1, 1)
        total[...] = part if at == 0 else total[...] + part
    return copies


def experts_kernel(x_ref, first_hbm, second_hbm, y_ref, pre_ref, first, second, total, sems):
    chunks = Chunks(first_hbm, second_hbm, first, second, sems)
    experts_forward_steps(chunks, x_ref[...], first, second, total, pre_ref)
    y_ref[...] = total[...].astype(LOW)


def experts_second_kernel(pre_ref, grad_ref, out_ref, gsecond, sems):
    hidden = gsecond.shape[1]
    copies = []
    for at in range(CHUNKS):
        act = gelu_of(pre_ref[at]).astype(LOW)
        gsecond[at] = dot_dims(act, grad_ref[...], 0, 0).astype(LOW)
        target = out_ref.at[at * hidden : (at + 1) * hidden]
        copies.append(pltpu.make_async_copy(gsecond.at[at], target, sems.at[at]))
        copies[-1].start()
    for one in copies:
        one.wait()


def experts_back_kernel(x_ref, grad_ref, pre_ref, first_hbm, second_hbm, dx_ref, out_first, *refs):
    first, second, total, gfirst, sems, out_sems = refs
    chunks = Chunks(first_hbm, second_hbm, first, second, sems)
    copies = experts_back_steps(
        x_ref[...],
        grad_ref[...],
        pre_ref,
        first,
        second,
        total,
        gfirst,
        None,
        (out_first, None),
        out_sems,
        chunks,
    )
    dx_ref[...] = total[...].astype(LOW)
    for one in copies:
        one.wait()


def experts_both_kernel(width, x_ref, cot_ref, *refs):
    first_hbm, second_hbm, y_ref, dx_ref, out_first, out_second = refs[:6]
    first, second, total, gfirst, gsecond, pre, sems, out_sems = refs[6:]
    chunks = Chunks(first_hbm, second_hbm, first, second, sems)
    x = x_ref[:, :width]
    experts_forward_steps(chunks, x, first, second, total, pre)
    y_low = total[...].astype(LOW)
    y_ref[...] = y_low
    cot = cot_ref[...].astype(WIDE)
    grad_gate = jnp.sum(y_low.astype(WIDE) * cot, axis=1, keepdims=True)
    high = grad_gate.astype(LOW).astype(WIDE)
    lane = lax.broadcasted_iota(jnp.int32, (x.shape[0], x_ref.shape[1] - width), 1)
    both = jnp.where(lane == 0, high, jnp.where(lane == 1, grad_gate - high, 0.0))
    dx_ref[:, width:] = both.astype(LOW)
    gate = x_ref[:, width : width + 1].astype(WIDE) + x_ref[:, width + 1 : width + 2].astype(WIDE)
    grad = (gate * cot).astype(LOW)
    copies = experts_back_steps(
        x, grad, pre, first, second, total, gfirst, gsecond, (out_first, out_second), out_sems, None
    )
    dx_ref[:, :width] = total[...].astype(LOW)
    for one in copies:
        one.wait()


def expert_call(kernel, arrays, first, second, shapes, with_grads, scratch):
    width, hidden = first.shape
    rows = arrays[0].shape[0]
    weights = [
        pltpu.VMEM((CHUNKS, width, hidden // CHUNKS), LOW),
        pltpu.VMEM((CHUNKS, hidden // CHUNKS, width), LOW),
    ]
    grads = [jax.ShapeDtypeStruct(one.shape, LOW) for one in (first, second)]
    sems = [pltpu.SemaphoreType.DMA((2, CHUNKS))]
    return pl.pallas_call(
        kernel,
        out_shape=(*shapes, *(grads if with_grads else [])),
        in_specs=[*in_vmem(len(arrays)), *any_specs(2)],
        out_specs=(*in_vmem(len(shapes)), *any_specs(2 if with_grads else 0)),
        scratch_shapes=[
            *weights,
            pltpu.VMEM((rows, width), WIDE),
            *(weights if with_grads else []),
            *scratch,
            *sems,
            *(sems if with_grads else []),
        ],
        compiler_params=pltpu.CompilerParams(vmem_limit_bytes=VMEM_BYTES),
    )(*arrays, first, second)


def pre_shape(rows, first):
    return (CHUNKS, rows, first.shape[1] // CHUNKS)


def run_experts(rows_in, first, second):
    shapes = [
        jax.ShapeDtypeStruct(rows_in.shape, LOW),
        jax.ShapeDtypeStruct(pre_shape(rows_in.shape[0], first), WIDE),
    ]
    return expert_call(experts_kernel, [rows_in], first, second, shapes, False, [])


def run_experts_second(pre, grad, second):
    hidden, width = second.shape
    return pl.pallas_call(
        experts_second_kernel,
        out_shape=jax.ShapeDtypeStruct(second.shape, LOW),
        in_specs=in_vmem(2),
        out_specs=any_specs(1)[0],
        scratch_shapes=[
            pltpu.VMEM((CHUNKS, hidden // CHUNKS, width), LOW),
            pltpu.SemaphoreType.DMA((CHUNKS,)),
        ],
        compiler_params=pltpu.CompilerParams(vmem_limit_bytes=VMEM_BYTES),
    )(pre, grad)


def run_experts_back(rows_in, grad, pre, first, second):
    width, hidden = first.shape
    weights = [
        pltpu.VMEM((CHUNKS, width, hidden // CHUNKS), LOW),
        pltpu.VMEM((CHUNKS, hidden // CHUNKS, width), LOW),
    ]
    return pl.pallas_call(
        experts_back_kernel,
        out_shape=[
            jax.ShapeDtypeStruct(rows_in.shape, LOW),
            jax.ShapeDtypeStruct(first.shape, LOW),
        ],
        in_specs=[*in_vmem(3), *any_specs(2)],
        out_specs=[*in_vmem(1), *any_specs(1)],
        scratch_shapes=[
            *weights,
            pltpu.VMEM(rows_in.shape, WIDE),
            weights[0],
            pltpu.SemaphoreType.DMA((2, CHUNKS)),
            pltpu.SemaphoreType.DMA((2, CHUNKS)),
        ],
        compiler_params=pltpu.CompilerParams(vmem_limit_bytes=VMEM_BYTES),
    )(rows_in, grad, pre, first, second)


def run_experts_both(rows_in, cot, first, second):
    kernel = functools.partial(experts_both_kernel, cot.shape[1])
    shapes = [jax.ShapeDtypeStruct(cot.shape, LOW), jax.ShapeDtypeStruct(rows_in.shape, LOW)]
    scratch = [pltpu.VMEM(pre_shape(cot.shape[0], first), WIDE)]
    return expert_call(kernel, [rows_in, cot], first, second, shapes, True, scratch)


def by_core(core, zero, one):
    return jnp.where(core == 0, zero, one)


def cut_kernel(words, first_ref, second_ref, first_mine, second_mine, first_sent, second_sent):
    first_mine[...] = first_ref[words[1]].astype(LOW)
    second_mine[...] = second_ref[words[1]].astype(LOW)
    first_sent[...] = first_ref[1 - words[1]].astype(LOW)
    second_sent[...] = second_ref[1 - words[1]].astype(LOW)


def cut_experts(words, first, second):
    shapes = [first.shape[1:], second.shape[1:]] * 2
    return pl.pallas_call(
        cut_kernel,
        out_shape=[jax.ShapeDtypeStruct(one, LOW) for one in shapes],
        in_specs=[pl.BlockSpec(memory_space=pltpu.SMEM), *in_vmem(2)],
        out_specs=in_vmem(4),
        compiler_params=pltpu.CompilerParams(vmem_limit_bytes=VMEM_BYTES),
    )(words, first, second)


def choose_kernel(count, words, *refs):
    zeros, ones, outs = refs[:count], refs[count : 2 * count], refs[2 * count :]

    def copy_all(sources):
        for source, out in zip(sources, outs):
            out[...] = source[...]

    @pl.when(words[1] == 0)
    def _():
        copy_all(zeros)

    @pl.when(words[1] != 0)
    def _():
        copy_all(ones)


def chosen_by_core(words, zeros, ones):
    count = len(zeros)
    return pl.pallas_call(
        functools.partial(choose_kernel, count),
        out_shape=[jax.ShapeDtypeStruct(one.shape, one.dtype) for one in zeros],
        in_specs=[pl.BlockSpec(memory_space=pltpu.SMEM), *in_vmem(2 * count)],
        out_specs=in_vmem(count),
        compiler_params=pltpu.CompilerParams(vmem_limit_bytes=VMEM_BYTES),
    )(words, *zeros, *ones)


def join_kernel(words, *refs):
    ones, twos, came, outs = refs[:2], refs[2:4], refs[4:6], refs[6:8]
    for at in range(2):
        outs[at][1 - words[1]] = came[at][...].astype(WIDE)

    @pl.when(words[1] == 0)
    def _():
        for at in range(2):
            outs[at][0] = ones[at][...].astype(WIDE)

    @pl.when(words[1] != 0)
    def _():
        for at in range(2):
            outs[at][1] = twos[at][...].astype(WIDE)


def join_experts(words, ones, twos, came):
    return pl.pallas_call(
        join_kernel,
        out_shape=[jax.ShapeDtypeStruct((2, *one.shape), WIDE) for one in ones],
        in_specs=[pl.BlockSpec(memory_space=pltpu.SMEM), *in_vmem(6)],
        out_specs=in_vmem(2),
        compiler_params=pltpu.CompilerParams(vmem_limit_bytes=VMEM_BYTES),
    )(words, *ones, *twos, *came)


def pack_kernel(words, small_ref, *refs):
    early_mine, early_sent, late_mine, late_sent = refs[4:]
    lead = small_ref.shape[1]
    early_mine[:, :lead] = small_ref[...]
    early_sent[:, :lead] = small_ref[...]
    for at, ref in enumerate(refs[:4]):
        half = ref.shape[1] // 2
        low, high = ref[:, :half], ref[:, half:]
        mine = by_core(words[1], low, high).astype(LOW)
        sent = by_core(words[1], high, low).astype(LOW)
        if at < 3:
            cols = slice(lead + at * half, lead + (at + 1) * half)
            early_mine[:, cols] = mine
            early_sent[:, cols] = sent
        else:
            late_mine[...] = mine
            late_sent[...] = sent


def pack_dense(words, small, weights):
    shard, width = weights[0].shape
    early, late = (shard, small.shape[1] + 3 * width // 2), (shard, width // 2)
    return pl.pallas_call(
        pack_kernel,
        out_shape=[jax.ShapeDtypeStruct(one, LOW) for one in (early, early, late, late)],
        in_specs=[pl.BlockSpec(memory_space=pltpu.SMEM), *in_vmem(5)],
        out_specs=in_vmem(4),
        compiler_params=pltpu.CompilerParams(vmem_limit_bytes=VMEM_BYTES),
    )(words, small, *weights)


def unpack_kernel(words, own_ref, came_ref, *outs):
    half = outs[0].shape[1] // 2
    for at, out in enumerate(outs[:4]):
        cols = slice(at * half, (at + 1) * half)
        own, came = own_ref[:, cols], came_ref[:, cols]
        out[:, :half] = by_core(words[1], own, came)
        out[:, half:] = by_core(words[1], came, own)
    outs[4][...] = own_ref[:, 4 * half :] + came_ref[:, 4 * half :]


def unpack_dense(words, own, came, width):
    shard = own.shape[0]
    shapes = [(shard, width)] * 4 + [(shard, own.shape[1] - 2 * width)]
    return pl.pallas_call(
        unpack_kernel,
        out_shape=[jax.ShapeDtypeStruct(one, WIDE) for one in shapes],
        in_specs=[pl.BlockSpec(memory_space=pltpu.SMEM), *in_vmem(2)],
        out_specs=in_vmem(5),
        compiler_params=pltpu.CompilerParams(vmem_limit_bytes=VMEM_BYTES),
    )(words, own, came)


def norm_back(grad_out, value, inverse, gain_row):
    scaled = grad_out * gain_row
    return inverse * (
        scaled - value * inverse * inverse * jnp.mean(scaled * value, axis=-1, keepdims=True)
    )


def sums_by_token_kernel(width, *refs):
    sent_ref, hot0, hot1, *more, out_ref = refs
    lanes = out_ref.shape[1] - width
    sent = sent_ref[:, :width]
    out_ref[:, :width] = dot_dims(hot0[...] + hot1[...], sent, 0, 0)
    lane = lax.broadcasted_iota(jnp.int32, (out_ref.shape[0], lanes), 1)
    parts = []
    for hot in (hot0, hot1):
        if more:
            returned_ref, grad_ref = more
            picked = dot_dims(hot[...], returned_ref[...], 0, 0)
            parts.append(jnp.sum(grad_ref[...].astype(WIDE) * picked, axis=1, keepdims=True))
        else:
            both = dot_dims(hot[...], sent_ref[:, width:], 0, 0)
            parts.append(both[:, :1] + both[:, 1:2])
    out_ref[:, width:] = jnp.where(lane == 0, parts[0], jnp.where(lane == 1, parts[1], 0.0))


def local_call(kernel, shapes, *arrays):
    def whole(one):
        if one.ndim == 1:
            return pl.BlockSpec(memory_space=pltpu.SMEM)
        return pl.BlockSpec(one.shape, lambda step: (0,) * one.ndim)

    return pl.pallas_call(
        kernel,
        grid=(1,),
        out_shape=shapes,
        in_specs=[whole(one) for one in arrays],
        out_specs=[whole(one) for one in shapes],
        compiler_params=pltpu.CompilerParams(vmem_limit_bytes=VMEM_BYTES),
    )(*arrays)


def column_sums(block, lanes, at):
    lane = lax.broadcasted_iota(jnp.int32, (block.shape[0], lanes), 1)
    return lax.dot_general(
        block,
        jnp.where(lane == at, 1.0, 0.0).astype(WIDE),
        (((0,), (0,)), ((), ())),
        precision=lax.Precision.HIGHEST,
        preferred_element_type=WIDE,
    )


def to_attention_kernel(words, *refs):
    mine_ref, other_ref, gates_ref, routes_ref, residual_ref, normed_ref, gain_ref = refs[:7]
    small_ref, out_w, grad_ref, dh_ref, attn_ref, branch_ref, grads_ref = refs[7:]
    width, lanes = residual_ref.shape[1], small_ref.shape[1]
    sums = mine_ref[...] + other_ref[...]
    grad_gates, gates = sums[:, width : width + 2], gates_ref[...]
    grad_chosen = gates * (grad_gates - jnp.sum(gates * grad_gates, axis=1, keepdims=True))
    routes = routes_ref[...]
    column = lax.broadcasted_iota(jnp.int32, (routes.shape[0], lanes), 1) - 2
    grad_logits = jnp.where(column == routes[:, :1], grad_chosen[:, :1], 0.0) + jnp.where(
        column == routes[:, 1:], grad_chosen[:, 1:2], 0.0
    )
    grad_logits = grad_logits.astype(LOW)
    grad_normed = sums[:, :width] + dot_dims(grad_logits, small_ref[...], 1, 1)
    residual = residual_ref[...]
    inverse = lax.rsqrt(jnp.mean(residual * residual, axis=1, keepdims=True) + EPS)
    grads_ref[...] = dot_dims(normed_ref[...], grad_logits, 0, 0) + column_sums(
        grad_normed * residual * inverse, lanes, 1
    )
    grad = grad_ref[...].astype(WIDE) + norm_back(grad_normed, residual, inverse, gain_ref[...])
    dh_ref[...] = grad
    low = grad.astype(LOW)
    half = branch_ref.shape[1]
    branch_ref[...] = by_core(words[1], low[:, :half], low[:, half:])
    heads = out_w[pl.ds(pl.multiple_of(words[1] * half, 16), half), :]
    attn_ref[...] = dot_dims(low, heads, 1, 1).astype(LOW)


def from_attention_kernel(count, *refs):
    query_ref, own_ref, *more = refs
    came, (weight_ref, qkv_ref, partial_ref) = more[:count], more[count:]
    half = query_ref.shape[1]
    total = own_ref[...]
    for one in came:
        total = total + one[...].astype(WIDE)
    qkv_ref[:, :half] = query_ref[...]
    qkv_ref[:, half:] = total.astype(LOW)
    partial_ref[...] = dot_dims(qkv_ref[...], weight_ref[...], 1, 1)


def to_input_kernel(mine_ref, other_ref, dh_ref, value_ref, gain_ref, small_ref, *refs):
    grad_normed = mine_ref[...] + other_ref[...]
    value = value_ref[...].astype(WIDE)
    inverse = lax.rsqrt(jnp.mean(value * value, axis=1, keepdims=True) + EPS)
    grad = dh_ref[...] + norm_back(grad_normed, value, inverse, gain_ref[...])
    grads_ref, out_ref, *slot_refs = refs[-2:] if len(refs) == 2 else refs[3:]
    grads_ref[...] = small_ref[...] + column_sums(
        grad_normed * value * inverse, grads_ref.shape[1], 0
    )
    out_ref[...] = grad
    if slot_refs:
        gates_ref, hot0, hot1 = refs[:3]
        low = grad.astype(LOW).astype(WIDE)
        rows = dot_wide(hot0[...], (gates_ref[:, :1] * low).astype(LOW))
        rows = rows + dot_wide(hot1[...], (gates_ref[:, 1:2] * low).astype(LOW))
        slot_refs[0][...] = rows.astype(LOW)


def body(
    inputs,
    cotangent,
    segments,
    buckets,
    routes,
    gain_attn,
    w_query,
    w_key,
    w_value,
    w_out,
    rel_bias,
    gain_moe,
    w_router,
    w_in,
    w_back,
):
    core = lax.axis_index("section")
    is_first = core == 0
    ctx_rank = lax.axis_index("ctx")
    ctx_count = lax.axis_size("ctx")
    exp_count = lax.axis_size("exp")
    held, rows, width = inputs.shape[0], inputs.shape[2], inputs.shape[3]
    groups = ctx_count // held
    parity = ctx_rank % held
    is_even = parity == 0
    group_rank = ctx_rank // held
    heads = rel_bias.shape[2]
    head_dim = width // heads
    half = width // 2
    half_heads = heads // 2
    local_exp = w_in.shape[1]
    experts = exp_count * local_exp
    capacity = 2 * rows // experts * 5 // 4
    bucket_count = rel_bias.shape[1] * ctx_count * exp_count
    shard = w_query.shape[1]
    rel_cols = rel_bias.shape[1] * heads // shard
    small_used = 2 + experts + rel_cols
    small_width = -(-small_used // 128) * 128
    extra = 128
    tokens = held * rows

    def regrouped(block):
        mine = lax.dynamic_index_in_dim(block, parity, 0, keepdims=False)
        sent = lax.dynamic_index_in_dim(block, 1 - parity, 0, keepdims=False)
        came = crossed(sent, 1)
        return jnp.where(is_even, jnp.stack([mine, came]), jnp.stack([came, mine]))

    def own_order(mine, other, axis):
        return jnp.where(
            is_first,
            jnp.concatenate([mine, other], axis=axis),
            jnp.concatenate([other, mine], axis=axis),
        )

    def both_cores(mine, axis=0):
        return own_order(mine, swapped(mine), axis)

    words = jnp.stack([ctx_rank, core]).astype(jnp.int32)
    small = jnp.concatenate(
        [
            gain_attn[0].astype(LOW)[:, None],
            gain_moe[0].astype(LOW)[:, None],
            w_router[0].astype(LOW),
            rel_bias[0].astype(LOW).reshape(shard, rel_cols),
            jnp.zeros((shard, small_width - small_used), LOW),
        ],
        axis=1,
    )

    def by_section(mine, other):
        return (jnp.where(is_first, mine, other), jnp.where(is_first, other, mine))

    first_mine, second_mine, first_sent, second_sent = cut_experts(words, w_in[0], w_back[0])
    own_shards, came_shards = [first_mine, second_mine], [swapped(first_sent), swapped(second_sent)]
    shards_one = chosen_by_core(words, own_shards, came_shards)
    early_mine, early_sent, late_mine, late_sent = pack_dense(
        tied(words, first_mine), small, [w[0] for w in (w_query, w_key, w_value, w_out)]
    )
    early_shards = by_section(early_mine, swapped(early_sent))
    late_shards = by_section(late_mine, swapped(late_sent))
    _, early_line = exp_line(early_shards[0])
    shards_two = chosen_by_core(words, came_shards, own_shards)

    def gathered(shards):
        return [lax.all_gather(one, "ctx", axis=0, tiled=True) for one in shards]

    seg_row = lax.dynamic_index_in_dim(segments[:, 0], parity, 0, keepdims=False)
    seg_blocks = seg_row.reshape(groups, held, rows)
    seg_keys = []
    for back in range(groups):
        seg = lax.dynamic_index_in_dim(
            seg_blocks, jnp.maximum(group_rank - back, 0), 0, keepdims=False
        )
        seg_keys.append(jnp.where(group_rank >= back, seg, -1))
    seg_q = seg_keys[0][:, :, None]
    seg_k = jnp.concatenate(seg_keys, axis=0)[:, None, :]

    back_order = jnp.flip(jnp.concatenate([jnp.broadcast_to(buckets[:1], (rows,)), buckets]))
    span = back_order.shape[0]
    by_distance = []
    for at in range(ctx_count):
        start = span - 2 * rows - at * rows
        by_distance.append(back_order[start : start + 2 * rows])
    bucket_vec = jnp.concatenate(by_distance)
    bucket_hot = (
        bucket_vec[:, None] == jnp.arange(bucket_count, dtype=jnp.int32)[None, :]
    ).astype(LOW)

    route_rows = regrouped(routes[:, 0])
    expert_ids = jnp.arange(experts, dtype=jnp.int32)
    flat_routes = route_rows.reshape(held, 2 * rows)
    member = (flat_routes[..., None] == expert_ids).astype(jnp.int32)
    slot_rank = jnp.sum((jnp.cumsum(member, axis=1) - member) * member, axis=-1)
    block_at = jnp.arange(held, dtype=jnp.int32)[:, None]
    slot_dest = ((flat_routes * held + block_at) * capacity + slot_rank).reshape(tokens, 2)
    exp_ids = jnp.arange(exp_count, dtype=jnp.int32)[:, None, None]
    in_block = block_at[None] * capacity + jnp.arange(capacity, dtype=jnp.int32)[None, None, :]
    slots = exp_count * held * capacity
    slot_ids = ((exp_ids * local_exp + core) * held * capacity + in_block).reshape(slots, 1)
    hots = [(slot_ids == slot_dest[None, :, c]).astype(LOW) for c in range(2)]
    to_token = hots[0] + hots[1]
    route_rows = route_rows.reshape(tokens, 2)
    small_ids = jnp.arange(small_width, dtype=jnp.int32)[None, :] - 2
    chosen_hot = [(route_rows[:, c : c + 1] == small_ids).astype(WIDE) for c in range(2)]

    def early_weights(early):
        tail = early[:, :small_width]
        rel = tail[:, 2 + experts : 2 + experts + rel_cols].reshape(bucket_count, heads)
        rel_mine = lax.dynamic_slice_in_dim(rel, core * half_heads, half_heads, 1)
        vec = dot_dims(rel_mine, bucket_hot, 0, 1)
        bias = bias_blocks(vec.reshape(half_heads, ctx_count, 1, 2 * rows), rows, ctx_count)
        return dict(
            qkv=early[:, small_width:],
            gain_a=tail[:, 0].astype(WIDE),
            gain_m=tail[:, 1].astype(WIDE),
            small=tail,
            bias=bias,
        )

    def late_weights(out_half):
        out_full = both_cores(out_half, 1)
        return dict(
            out=out_full, out_mine=lax.dynamic_slice_in_dim(out_full, core * half, half, 0)
        )

    def to_experts(rows_out):
        lanes = rows_out.shape[1]
        return lax.all_to_all(
            rows_out.reshape(exp_count, held * capacity, lanes),
            "exp",
            split_axis=0,
            concat_axis=0,
            tiled=True,
        ).reshape(slots, lanes)

    def in_two(wide):
        high = wide.astype(LOW)
        low = (wide - high.astype(WIDE)).astype(LOW)
        pad = jnp.zeros((wide.shape[0], extra - 2), LOW)
        return jnp.concatenate([high, low, pad], axis=1)

    def normed(value, gain_row):
        inverse = lax.rsqrt(jnp.mean(value * value, axis=-1, keepdims=True) + EPS)
        return (value * inverse * gain_row).astype(LOW), inverse

    def attention(normed_a, weights, arrived, arrived_after):
        qkv = dot_wide(normed_a, weights["qkv"]).astype(LOW)
        query, kv = qkv[:, :half], tied(qkv[:, half:], *arrived)
        kv_groups = [kv] + [shifted(kv, held * back) for back in range(1, groups)]
        attn_wide, attn_mine, log_total = attend(
            query, kv_groups, weights["bias"], seg_q, seg_k, rows, head_dim
        )
        attn_low = both_cores(tied(attn_mine, *arrived_after), 1)
        return dict(
            normed_a=normed_a,
            query=query,
            kv_groups=kv_groups,
            attn_wide=attn_wide,
            attn_low=attn_low,
            log_total=log_total,
        )

    def forward_to_experts(value, kept, weights, with_gates, arrived):
        residual = value + dot_wide(kept["attn_low"], weights["out"])
        normed_m, inv_m = normed(residual, weights["gain_m"])
        logits = dot_wide(normed_m, weights["small"])
        chosen = [jnp.sum(logits * hot_c, axis=-1, keepdims=True) for hot_c in chosen_hot]
        gates = jax.nn.softmax(jnp.concatenate(chosen, axis=1), axis=-1)
        sent = dot_wide(to_token, normed_m).astype(LOW)
        if with_gates:
            gate_rows = dot_wide(hots[0], in_two(gates[:, :1])) + dot_wide(
                hots[1], in_two(gates[:, 1:])
            )
            sent = jnp.concatenate([sent, gate_rows.astype(LOW)], axis=1)
        received = to_experts(tied(sent, *arrived))
        return dict(
            kept,
            value=value,
            residual=residual,
            inv_m=inv_m,
            normed_m=normed_m,
            gates=gates,
            received=received,
        )

    def combined(produced, kept):
        returned = to_experts(produced)
        picked = [dot_dims(hot_c, returned, 0, 0) for hot_c in hots]
        partial = kept["gates"][:, :1] * picked[0] + kept["gates"][:, 1:] * picked[1]
        return kept["residual"] + (partial + swapped(partial)), returned

    def wide_like(*shape):
        return jax.ShapeDtypeStruct(shape, WIDE)

    def low_like(*shape):
        return jax.ShapeDtypeStruct(shape, LOW)

    def backward_from_experts(grad_out, grad_sent, returned, weights, kept, below, arrived=()):
        more = [] if returned is None else [returned, grad_out]
        (partial,) = local_call(
            functools.partial(sums_by_token_kernel, width),
            [wide_like(tokens, width + extra)],
            grad_sent,
            *hots,
            *more,
        )
        grad_residual, grad_attn, branch_mine, small_part = local_call(
            to_attention_kernel,
            [
                wide_like(tokens, width),
                low_like(tokens, half),
                low_like(tokens, half),
                wide_like(width, small_width),
            ],
            words,
            partial,
            swapped(partial),
            kept["gates"],
            route_rows,
            kept["residual"],
            kept["normed_m"],
            weights["gain_m"][None],
            weights["small"],
            weights["out"],
            grad_out,
        )
        back = attend_back(
            kept["query"],
            kept["kv_groups"],
            weights["bias"],
            seg_q,
            seg_k,
            kept["log_total"],
            grad_attn,
            kept["attn_wide"],
            rows,
            head_dim,
        )
        grad_query, diag = tied(back[0], *arrived), back[-1]
        came = [shifted(back[1 + at], -held * at) for at in range(1, groups)]
        grad_qkv, partial = local_call(
            functools.partial(from_attention_kernel, groups - 1),
            [low_like(tokens, 3 * half), wide_like(tokens, width)],
            grad_query,
            back[1],
            *came,
            weights["qkv"],
        )
        slot_inputs = [] if below is None else [below, *hots]
        small_part, grad_value, *slot_rows = local_call(
            to_input_kernel,
            [wide_like(width, small_width), wide_like(tokens, width)]
            + ([] if below is None else [low_like(slots, width)]),
            partial,
            swapped(partial),
            grad_residual,
            kept["low"],
            weights["gain_a"][None],
            small_part,
            *slot_inputs,
        )
        grad_rel = lax.dot_general(
            bucket_hot.astype(WIDE),
            diag.reshape(half_heads, -1),
            (((0,), (1,)), ((), ())),
            precision=lax.Precision.HIGHEST,
            preferred_element_type=WIDE,
        )
        grad_rel = own_order(grad_rel, jnp.zeros_like(grad_rel), 1)
        rel_columns = jnp.pad(
            grad_rel.reshape(width, rel_cols),
            ((0, 0), (2 + experts, small_width - small_used)),
        )
        small_grads = (0.5 * small_part + rel_columns).astype(LOW)
        grads_of = (kept["normed_a"], grad_qkv, kept["attn_low"], branch_mine, small_grads)
        return grad_value, grads_of, grad_qkv, grad_attn, slot_rows

    def whole_dense_grads(normed_a, grad_qkv, attn_low, branch, small):
        qkv_w, out_w = dot_dims(normed_a, grad_qkv, 0, 0), dot_dims(attn_low, branch, 0, 0)
        return scattered_rows(
            jnp.concatenate([qkv_w.astype(LOW), out_w.astype(LOW), small], axis=1)
        )

    def summed_shards(grads):
        return [
            lax.psum_scatter(one, "ctx", scatter_dimension=0, tiled=True) for one in grads
        ]

    relayed = four_by_four()
    both = jnp.concatenate([early_shards[1], late_shards[1]], axis=1)
    if relayed:
        plane = plane_rows(both)
        planes = [plane] + sent_along_exp([plane] * 4)
        both = all_rows(planes, shard)
        early_line = tied(early_line, plane)
    else:
        planes = [both] * 4
        both = lax.all_gather(both, ("ctx", "exp"), axis=0, tiled=True)
    _, late_line = exp_line(tied(late_shards[0], early_line))
    early_one = tied(ctx_rows(early_line, []), late_line)
    dense_one = early_weights(early_one)
    value_low = regrouped(inputs[:, 0]).reshape(tokens, width)
    value = value_low.astype(WIDE)
    normed_a, inv_a = normed(value, dense_one["gain_a"])
    cot = regrouped(cotangent[:, 0]).reshape(tokens, width)
    experts_one = gathered(shards_one)
    kept_one = attention(normed_a, dense_one, [planes[1]], [planes[2]])
    kv_came = kept_one["kv_groups"][-1]
    dense_one = dict(dense_one, **late_weights(ctx_rows(late_line, [kv_came])))
    kept_one = forward_to_experts(value, kept_one, dense_one, False, [])
    kept_one["low"] = value_low
    experts_two = gathered([tied(one, kept_one["received"]) for one in shards_two])
    produced, pre_one = run_experts(kept_one["received"], *experts_one)
    out_one, returned_one = combined(tied(produced, planes[3]), kept_one)

    dense_two = dict(
        early_weights(both[:, : small_width + 3 * half]),
        **late_weights(both[:, small_width + 3 * half :]),
    )
    value_low = out_one.astype(LOW)
    value = value_low.astype(WIDE)
    normed_a, inv_a = normed(value, dense_two["gain_a"])
    kept_two = attention(normed_a, dense_two, [], [])
    cot_rows = to_experts(tied(dot_wide(to_token, cot).astype(LOW), out_one))
    kept_two = forward_to_experts(value, kept_two, dense_two, True, [cot_rows])
    kept_two["low"] = value_low
    produced, grad_rows, *grads_two = run_experts_both(
        kept_two["received"], cot_rows, *experts_two
    )
    grad_sent = to_experts(grad_rows)
    sums_two = summed_shards(grads_two)
    grad_two, grads_of_two, _, grad_attn, (slot_rows,) = backward_from_experts(
        cot, grad_sent, None, dense_two, kept_two, kept_one["gates"]
    )
    out_two, _ = combined(tied(produced, grad_attn), kept_two)

    grad_out = grad_two.astype(LOW)
    grad_rows = to_experts(slot_rows)
    if relayed:
        early_parts, late_parts = dense_grads(*grads_of_two)
        grad_rows = tied(grad_rows, *late_parts, *early_parts)
        early_hop = first_hop(early_parts, 2, 1)
    grad_rows, out_two = lax.optimization_barrier((grad_rows, out_two))
    second_grads = run_experts_second(pre_one, grad_rows, experts_one[1])
    sums_one = summed_shards([second_grads])
    grad_rows, first_grads = run_experts_back(
        kept_one["received"], grad_rows, tied(pre_one, second_grads), *experts_one
    )
    sums_one = summed_shards([first_grads]) + sums_one
    activations = regrouped(jnp.where(is_first, out_one, out_two).reshape(held, rows, width))
    grad_sent = to_experts(grad_rows)
    late_two, early_two = [], []
    if relayed:
        grad_sent, early_hop = lax.optimization_barrier((grad_sent, early_hop))
        late_two = sent_along_exp([tied(one, grad_sent) for one in late_parts])
        early_two = [finished_along_exp(last_hop(early_hop, 1))]
    grad_one, grads_of_one, grad_qkv, _, _ = backward_from_experts(
        grad_out, grad_sent, returned_one, dense_one, kept_one, None, [*late_two, *early_two]
    )
    came = [swapped(one) for one in chosen_by_core(words, sums_two, sums_one)]
    if relayed:
        late_parts_two = late_parts
        early_parts, late_parts = dense_grads(*grads_of_one)
        late_two = [tied(one, late_parts[0]) for one in late_two]
        late_one = sent_along_exp(late_parts)
        early_one = over_ctx(early_parts)
        dense_sum_one = jnp.concatenate(
            [finished_along_exp(early_one), finished_along_ctx(late_parts, late_one)], axis=1
        )
        dense_sum_two = jnp.concatenate(
            [early_two[0], finished_along_ctx(late_parts_two, late_two)], axis=1
        )
    else:
        dense_sum_two = whole_dense_grads(*grads_of_two)
        dense_sum_one = whole_dense_grads(*grads_of_one)

    grads_in = regrouped(jnp.where(is_first, grad_one, grad_two).reshape(held, rows, width))
    dense_own = jnp.where(is_first, dense_sum_one, dense_sum_two)
    dense_came = swapped(jnp.where(is_first, dense_sum_two, dense_sum_one))
    dense_own, *came = lax.optimization_barrier((dense_own, *came))
    query_out, key_out, value_out, outproj_out, tail = unpack_dense(
        words, dense_own, dense_came, width
    )
    rel_out = tail[:, 2 + experts : 2 + experts + rel_cols].reshape(rel_bias.shape)
    first_out, second_out = join_experts(words, sums_one, sums_two, came)
    out_shape = (1, held, 1, rows, width)
    return (
        activations.reshape(out_shape),
        grads_in.reshape(out_shape),
        tail[:, 0][None],
        query_out[None],
        key_out[None],
        value_out[None],
        outproj_out[None],
        rel_out,
        tail[:, 1][None],
        tail[:, 2 : 2 + experts][None],
        first_out[None],
        second_out[None],
    )


def solution(mesh):
    rows_spec = P("section", ("ctx", "exp"), None)
    gain_spec = P("section", ("ctx", "exp"))
    expert_spec = P("section", "exp", "ctx", None)
    token_spec = P(None, "exp", "ctx", None)
    state_spec = P("section", None, "exp", "ctx", None)
    in_specs = (
        token_spec,
        token_spec,
        P(None, "exp", None),
        P(),
        token_spec,
        gain_spec,
        *[rows_spec] * 5,
        gain_spec,
        rows_spec,
        *[expert_spec] * 2,
    )
    out_specs = (
        *[state_spec] * 2,
        gain_spec,
        *[rows_spec] * 5,
        gain_spec,
        rows_spec,
        *[expert_spec] * 2,
    )
    return jax.shard_map(body, mesh=mesh, in_specs=in_specs, out_specs=out_specs, check_vma=False)
```

```python
import functools

import jax
import jax.numpy as jnp
from jax import lax
from jax.experimental import pallas as pl
from jax.experimental.pallas import tpu as pltpu
from jax.sharding import PartitionSpec as P

EPS = 1e-06
NEG = -1e30
LOW = jnp.bfloat16
WIDE = jnp.float32
VMEM_BYTES = 48 * 1024 * 1024


def swapped(block):
    return lax.ppermute(block, "section", [(0, 1), (1, 0)])


def shifted(block, distance):
    size = lax.axis_size("ctx")
    route = [(i, i + distance) for i in range(size) if 0 <= i + distance < size]
    return lax.ppermute(block, "ctx", route)


def crossed(block, bits, axis="ctx"):
    return lax.ppermute(block, axis, [(i, i ^ bits) for i in range(lax.axis_size(axis))])


def tied(value, *others):
    return lax.optimization_barrier((value, *others))[0]


def place_kernel(moves, count, rank_ref, *refs):
    out_ref, sems = refs[count:]
    copies = []
    for number, (at, first, size, fixed, relation) in enumerate(moves):
        start = fixed + (rank_ref[0] ^ relation) * size
        target = out_ref.at[pl.ds(pl.multiple_of(start, 16), size)]
        copies.append(
            pltpu.make_async_copy(refs[at].at[pl.ds(first, size)], target, sems.at[number])
        )
        copies[-1].start()
    for one in copies:
        one.wait()


def placed(rank, pieces, moves, rows):
    return pl.pallas_call(
        functools.partial(place_kernel, moves, len(pieces)),
        out_shape=jax.ShapeDtypeStruct((rows, pieces[0].shape[1]), pieces[0].dtype),
        in_specs=[
            pl.BlockSpec(memory_space=pltpu.SMEM),
            *[pl.BlockSpec(memory_space=pl.ANY)] * len(pieces),
        ],
        out_specs=in_vmem(1)[0],
        scratch_shapes=[pltpu.SemaphoreType.DMA((len(moves),))],
        compiler_params=pltpu.CompilerParams(vmem_limit_bytes=VMEM_BYTES),
    )(rank.reshape(1), *pieces)


def four_by_four():
    return lax.axis_size("ctx") == 4 and lax.axis_size("exp") == 4


def exp_line(block):
    if not four_by_four():
        return [block] * 2, lax.all_gather(block, "exp", axis=0, tiled=True)
    shard = block.shape[0]
    along_exp = [block] + [crossed(block, k, "exp") for k in (1, 2, 3)]
    moves = [(k, 0, shard, 0, k) for k in range(4)]
    return along_exp, placed(lax.axis_index("exp"), along_exp, moves, 4 * shard)


def ctx_rows(line, before_relay):
    if not four_by_four():
        return lax.all_gather(line, "ctx", axis=0, tiled=True)
    from_x, from_y = crossed(line, 1), crossed(line, 2)
    along_ctx = [line, from_x, from_y, crossed(tied(from_x, *before_relay), 2)]
    size = line.shape[0]
    moves = [(k, 0, size, 0, k) for k in range(4)]
    return placed(lax.axis_index("ctx"), along_ctx, moves, 4 * size)


def plane_rows(block):
    from_x, from_y = crossed(block, 1), crossed(block, 2)
    along_ctx = [block, from_x, from_y, crossed(from_x, 2)]
    shard = block.shape[0]
    moves = [(k, 0, shard, 0, k) for k in range(4)]
    return placed(lax.axis_index("ctx"), along_ctx, moves, 4 * shard)


def all_rows(planes, shard):
    moves = [(k, at * shard, shard, at * 4 * shard, k) for k in range(4) for at in range(4)]
    return placed(lax.axis_index("exp"), planes, moves, 16 * shard)


def added(left, right):
    return left.astype(WIDE) + right.astype(WIDE)


def first_hop(parts, near, far):
    relayed = added(parts[far], crossed(parts[3], near)).astype(LOW)
    return added(parts[0], crossed(parts[near], near)), relayed


def last_hop(state, far):
    mine, relayed = state
    return mine + crossed(relayed, far).astype(WIDE)


def parts_for(blocks, axis, name):
    rank = lax.axis_index(name)
    return [lax.dynamic_index_in_dim(blocks, rank ^ k, axis, keepdims=False) for k in range(4)]


def over_exp(parts, came):
    total = parts[0].astype(WIDE)
    for one in came:
        total = total + one.astype(WIDE)
    return total


def over_ctx(parts):
    return last_hop(first_hop(parts, 2, 1), 1)


def sent_along_exp(parts):
    return [crossed(parts[k], k, "exp") for k in (1, 2, 3)]


def finished_along_ctx(parts, came):
    return over_ctx(parts_for(over_exp(parts, came).astype(LOW), 0, "ctx"))


def finished_along_exp(part):
    shard = part.shape[0] // 4
    parts = parts_for(part.astype(LOW).reshape(4, shard, part.shape[1]), 0, "exp")
    return over_exp(parts, sent_along_exp(parts))


def scattered_rows(block):
    block = lax.psum_scatter(block, "ctx", scatter_dimension=0, tiled=True)
    return lax.psum_scatter(block, "exp", scatter_dimension=0, tiled=True).astype(WIDE)


def dense_grads_kernel(ranks, normed_ref, grad_ref, attn_ref, branch_ref, small_ref, *refs):
    early_outs, late_outs, early, late = refs[:4], refs[4:8], refs[8], refs[9]
    cut, half = early.shape[1], branch_ref.shape[1]
    rest = grad_ref.shape[1] - cut
    early[...] = dot_dims(normed_ref[...], grad_ref[:, :cut], 0, 0).astype(LOW)
    late[:, :rest] = dot_dims(normed_ref[...], grad_ref[:, cut:], 0, 0).astype(LOW)
    late[:, rest : rest + half] = dot_dims(attn_ref[...], branch_ref[...], 0, 0).astype(LOW)
    late[:, rest + half :] = small_ref[...]
    shard = early.shape[0] // 16

    def rows_at(start):
        return pl.ds(pl.multiple_of(start, 16), shard)

    for k in range(4):
        at_exp = (ranks[1] ^ k) * shard
        for at in range(4):
            late_outs[k][at] = late[rows_at(at * 4 * shard + at_exp), :]
            start = (ranks[0] ^ k) * 4 * shard + at * shard
            early_outs[k][at * shard : (at + 1) * shard] = early[rows_at(start), :]


def dense_grads(normed_a, grad_qkv, attn_low, branch, small):
    width, half = normed_a.shape[1], branch.shape[1]
    shard = width // 16
    late_columns = half + half + small.shape[1]
    shapes = [(4 * shard, 2 * half)] * 4 + [(4, shard, late_columns)] * 4
    ranks = jnp.stack([lax.axis_index("ctx"), lax.axis_index("exp")]).astype(jnp.int32)
    out = pl.pallas_call(
        dense_grads_kernel,
        out_shape=[jax.ShapeDtypeStruct(one, LOW) for one in shapes],
        in_specs=[pl.BlockSpec(memory_space=pltpu.SMEM), *in_vmem(5)],
        out_specs=in_vmem(8),
        scratch_shapes=[pltpu.VMEM((width, 2 * half), LOW), pltpu.VMEM((width, late_columns), LOW)],
        compiler_params=pltpu.CompilerParams(vmem_limit_bytes=VMEM_BYTES),
    )(ranks, normed_a, grad_qkv, attn_low, branch, small)
    return out[:4], out[4:]


def in_vmem(count):
    return [pl.BlockSpec(memory_space=pltpu.VMEM)] * count


def dot_wide(left, right):
    return jnp.dot(left, right, preferred_element_type=WIDE)


def dot_dims(left, right, left_dim, right_dim):
    return lax.dot_general(
        left, right, (((left_dim,), (right_dim,)), ((), ())), preferred_element_type=WIDE
    )


def bias_kernel(rows, blocks, vec_ref, out_ref):
    for head in range(vec_ref.shape[0]):
        for at in range(blocks):
            wide = jnp.broadcast_to(vec_ref[head, at], (rows, 2 * rows))
            turned = pltpu.roll(wide, rows + 1, 1, stride=1, stride_axis=0)
            out_ref[
                head // 2, pl.ds((head % 2) * rows, rows), pl.ds(at * rows, rows)
            ] = turned[:, :rows]


def bias_blocks(vec, rows, blocks):
    heads = vec.shape[0]
    return pl.pallas_call(
        functools.partial(bias_kernel, rows, blocks),
        out_shape=jax.ShapeDtypeStruct((heads // 2, 2 * rows, blocks * rows), WIDE),
        in_specs=in_vmem(1),
        out_specs=in_vmem(1)[0],
        compiler_params=pltpu.CompilerParams(vmem_limit_bytes=VMEM_BYTES),
    )(vec)


def mask_rows(rows, at_q, key_blocks, seg_q, segk_ref):
    parts = []
    for back, at_k in enumerate(key_blocks):
        seg_k = segk_ref[at_k]
        good = (seg_k == 0) | (seg_k == seg_q)
        if back == 0:
            q_at = lax.broadcasted_iota(jnp.int32, (rows, rows), 0)
            k_at = lax.broadcasted_iota(jnp.int32, (rows, rows), 1)
            good = good & (q_at >= k_at)
        parts.append(jnp.where(good, 0.0, NEG).astype(WIDE))
    one = jnp.concatenate(parts, axis=1)
    return jnp.concatenate([one, one], axis=0)


def stacked_pair(block, half):
    lane = lax.broadcasted_iota(jnp.int32, block.shape, 1)
    zero = jnp.zeros_like(block)
    return jnp.concatenate(
        [jnp.where(lane < half, block, zero), jnp.where(lane >= half, block, zero)], axis=0
    )


def unstacked_pair(block, half):
    rows = block.shape[0] // 2
    lane = lax.broadcasted_iota(jnp.int32, (rows, block.shape[1]), 1)
    return jnp.where(lane < half, block[:rows], block[rows:])


def key_order(at_q, held, groups):
    near = [(0, at) for at in range(at_q, -1, -1)]
    return near + [(group, at) for group in range(1, groups) for at in range(held - 1, -1, -1)]


def attend_kernel(held, rows, groups, head_dim, *refs):
    q_ref, kv_refs = refs[0], refs[1 : 1 + groups]
    bias_ref, segq_ref, segk_ref, wide_ref, low_ref, log_ref = refs[1 + groups :]
    pairs = bias_ref.shape[0]
    lanes = 2 * head_dim
    width = pairs * lanes
    for at_q in range(held):
        order = key_order(at_q, held, groups)
        mask = mask_rows(rows, at_q, [g * held + at for g, at in order], segq_ref[at_q], segk_ref)
        here = pl.ds(at_q * rows, rows)
        for pair in range(pairs):
            cols = pl.ds(pair * lanes, lanes)
            vcols = pl.ds(width + pair * lanes, lanes)
            query = stacked_pair(q_ref[here, cols] * (head_dim**-0.5), head_dim)
            keys = jnp.concatenate(
                [kv_refs[g][pl.ds(at * rows, rows), cols] for g, at in order], axis=0
            )
            values = jnp.concatenate(
                [kv_refs[g][pl.ds(at * rows, rows), vcols] for g, at in order], axis=0
            )
            bias = bias_ref[pair, :, pl.ds(0, len(order) * rows)]
            scores = dot_dims(query, keys, 1, 1) + bias + mask
            top = jnp.max(scores, axis=1, keepdims=True)
            weights = jnp.exp(scores - top)
            total = jnp.sum(weights, axis=1, keepdims=True)
            out = dot_wide(weights.astype(LOW), values) / total
            log_ref[at_q * pairs + pair] = top + jnp.log(total)
            out = unstacked_pair(out, head_dim)
            wide_ref[here, cols] = out
            low_ref[here, cols] = out.astype(LOW)


def attend(query, kv_groups, bias, seg_q, seg_k, rows, head_dim):
    groups = len(kv_groups)
    held = query.shape[0] // rows
    pairs = bias.shape[0]
    return pl.pallas_call(
        functools.partial(attend_kernel, held, rows, groups, head_dim),
        out_shape=(
            jax.ShapeDtypeStruct(query.shape, WIDE),
            jax.ShapeDtypeStruct(query.shape, LOW),
            jax.ShapeDtypeStruct((held * pairs, 2 * rows, 1), WIDE),
        ),
        in_specs=in_vmem(4 + groups),
        out_specs=tuple(in_vmem(3)),
        compiler_params=pltpu.CompilerParams(vmem_limit_bytes=VMEM_BYTES),
    )(query, *kv_groups, bias, seg_q, seg_k)


def diagonal_sums(block):
    rows = block.shape[0]
    wide = jnp.concatenate([block, jnp.zeros_like(block)], axis=1)
    while rows > 8:
        rows //= 2
        wide = pltpu.roll(wide[:rows], rows, 1) + wide[rows:]
    row_at = lax.broadcasted_iota(jnp.int32, wide.shape, 0)
    for step in (4, 2, 1):
        wide = jnp.where(((7 - row_at) & step) != 0, pltpu.roll(wide, step, 1), wide)
    return jnp.sum(wide, axis=0, keepdims=True)


def attend_back_kernel(held, rows, groups, head_dim, *refs):
    q_ref, kv_refs = refs[0], refs[1 : 1 + groups]
    bias_ref, segq_ref, segk_ref, log_ref, grad_ref, wide_ref = refs[1 + groups : 7 + groups]
    dq_ref, dkv_refs = refs[7 + groups], refs[8 + groups : 8 + 2 * groups]
    diag_ref, acc_ref, dkv_acc = refs[8 + 2 * groups :]
    pairs = bias_ref.shape[0]
    lanes = 2 * head_dim
    width = pairs * lanes
    scale = head_dim**-0.5
    seen = set()

    def add_to(group, at, cols, block):
        here = pl.ds(at * rows, rows)
        if (group, at, cols.start) in seen:
            dkv_acc[group, here, cols] += block
        else:
            seen.add((group, at, cols.start))
            dkv_acc[group, here, cols] = block

    for at_q in range(held - 1, -1, -1):
        order = key_order(at_q, held, groups)
        mask = mask_rows(rows, at_q, [g * held + at for g, at in order], segq_ref[at_q], segk_ref)
        here = pl.ds(at_q * rows, rows)
        for pair in range(pairs):
            cols = pl.ds(pair * lanes, lanes)
            vcols = pl.ds(width + pair * lanes, lanes)
            query = stacked_pair(q_ref[here, cols] * scale, head_dim)
            grad = stacked_pair(grad_ref[here, cols], head_dim)
            wide = stacked_pair(wide_ref[here, cols], head_dim)
            delta = jnp.sum(grad.astype(WIDE) * wide, axis=1, keepdims=True)
            keys = jnp.concatenate(
                [kv_refs[g][pl.ds(at * rows, rows), cols] for g, at in order], axis=0
            )
            values = jnp.concatenate(
                [kv_refs[g][pl.ds(at * rows, rows), vcols] for g, at in order], axis=0
            )
            span = pl.ds(0, len(order) * rows)
            scores = dot_dims(query, keys, 1, 1) + bias_ref[pair, :, span] + mask
            probs = jnp.exp(scores - log_ref[at_q * pairs + pair])
            grad_probs = dot_dims(grad, values, 1, 1)
            grad_scores = (probs * (grad_probs - delta)).astype(LOW)
            grad_query = unstacked_pair(dot_wide(grad_scores, keys) * scale, head_dim)
            dq_ref[here, cols] = grad_query.astype(LOW)
            grad_keys = dot_dims(grad_scores, query, 0, 0)
            grad_values = dot_dims(probs.astype(LOW), grad, 0, 0)
            for back, (group, at) in enumerate(order):
                part = slice(back * rows, (back + 1) * rows)
                add_to(group, at, cols, grad_keys[part])
                add_to(group, at, vcols, grad_values[part])
            if at_q == held - 1:
                acc_ref[pair] = grad_scores.astype(WIDE)
            else:
                acc_ref[pair, :, span] += grad_scores.astype(WIDE)
    for group in range(groups):
        dkv_refs[group][...] = dkv_acc[group].astype(dkv_refs[group].dtype)
    for pair in range(pairs):
        for head in range(2):
            for at in range(held * groups):
                block = acc_ref[pair, pl.ds(head * rows, rows), pl.ds(at * rows, rows)]
                diag_ref[2 * pair + head, at] = diagonal_sums(block)


def attend_back(query, kv_groups, bias, seg_q, seg_k, log_total, grad, wide, rows, head_dim):
    groups = len(kv_groups)
    held = query.shape[0] // rows
    pairs = bias.shape[0]
    kv_shape = kv_groups[0].shape
    return pl.pallas_call(
        functools.partial(attend_back_kernel, held, rows, groups, head_dim),
        out_shape=(
            jax.ShapeDtypeStruct(query.shape, LOW),
            jax.ShapeDtypeStruct(kv_shape, WIDE),
            *[jax.ShapeDtypeStruct(kv_shape, LOW)] * (groups - 1),
            jax.ShapeDtypeStruct((2 * pairs, held * groups, 1, 2 * rows), WIDE),
        ),
        in_specs=in_vmem(7 + groups),
        out_specs=tuple(in_vmem(2 + groups)),
        scratch_shapes=[pltpu.VMEM(bias.shape, WIDE), pltpu.VMEM((groups, *kv_shape), WIDE)],
        compiler_params=pltpu.CompilerParams(vmem_limit_bytes=VMEM_BYTES),
    )(query, *kv_groups, bias, seg_q, seg_k, log_total, grad, wide)


GELU_A = 0.7978845608028654
GELU_B = 0.044715


def gelu_of(pre):
    return 0.5 * pre * (1.0 + jnp.tanh(GELU_A * (pre + GELU_B * pre * pre * pre)))


def gelu_and_slope(pre):
    square = pre * pre
    bent = jnp.tanh(GELU_A * pre * (1.0 + GELU_B * square))
    half_up = 0.5 * (1.0 + bent)
    slope = half_up + 0.5 * pre * (1.0 - bent * bent) * (
        GELU_A * (1.0 + 3.0 * GELU_B * square)
    )
    return pre * half_up, slope


def any_specs(count):
    return [pl.BlockSpec(memory_space=pl.ANY)] * count


CHUNKS = 4


class Chunks:
    def __init__(self, first_hbm, second_hbm, first, second, sems):
        hidden = second.shape[1]
        self.first_copies = [
            pltpu.make_async_copy(
                first_hbm.at[:, at * hidden : (at + 1) * hidden], first.at[at], sems.at[0, at]
            )
            for at in range(CHUNKS)
        ]
        self.second_copies = [
            pltpu.make_async_copy(
                second_hbm.at[at * hidden : (at + 1) * hidden], second.at[at], sems.at[1, at]
            )
            for at in range(CHUNKS)
        ]
        for first_copy, second_copy in zip(self.first_copies, self.second_copies):
            first_copy.start()
            second_copy.start()


def experts_forward_steps(chunks, x, first, second, total, pre_ref):
    for at in range(CHUNKS):
        chunks.first_copies[at].wait()
        pre = dot_wide(x, first[at])
        pre_ref[at] = pre
        act = gelu_of(pre).astype(LOW)
        chunks.second_copies[at].wait()
        part = dot_wide(act, second[at])
        total[...] = part if at == 0 else total[...] + part


def experts_back_steps(x, grad, pre_ref, first, second, total, gfirst, gsecond, outs, sems, chunks):
    out_first, out_second = outs
    hidden = second.shape[1]
    copies = []
    for at in range(CHUNKS):
        if chunks is not None:
            chunks.second_copies[at].wait()
            chunks.first_copies[at].wait()
        here = slice(at * hidden, (at + 1) * hidden)
        act, slope = gelu_and_slope(pre_ref[at])
        if gsecond is not None:
            gsecond[at] = dot_dims(act.astype(LOW), grad, 0, 0).astype(LOW)
            copies.append(
                pltpu.make_async_copy(gsecond.at[at], out_second.at[here], sems.at[1, at])
            )
            copies[-1].start()
        grad_act = dot_dims(grad, second[at], 1, 1)
        grad_pre = (grad_act * slope).astype(LOW)
        gfirst[at] = dot_dims(x, grad_pre, 0, 0).astype(LOW)
        copies.append(pltpu.make_async_copy(gfirst.at[at], out_first.at[:, here], sems.at[0, at]))
        copies[-1].start()
        part = dot_dims(grad_pre, first[at], 1, 1)
        total[...] = part if at == 0 else total[...] + part
    return copies


def experts_kernel(x_ref, first_hbm, second_hbm, y_ref, pre_ref, first, second, total, sems):
    chunks = Chunks(first_hbm, second_hbm, first, second, sems)
    experts_forward_steps(chunks, x_ref[...], first, second, total, pre_ref)
    y_ref[...] = total[...].astype(LOW)


def experts_second_kernel(pre_ref, grad_ref, out_ref, gsecond, sems):
    hidden = gsecond.shape[1]
    copies = []
    for at in range(CHUNKS):
        act = gelu_of(pre_ref[at]).astype(LOW)
        gsecond[at] = dot_dims(act, grad_ref[...], 0, 0).astype(LOW)
        target = out_ref.at[at * hidden : (at + 1) * hidden]
        copies.append(pltpu.make_async_copy(gsecond.at[at], target, sems.at[at]))
        copies[-1].start()
    for one in copies:
        one.wait()


def experts_back_kernel(x_ref, grad_ref, pre_ref, first_hbm, second_hbm, dx_ref, out_first, *refs):
    first, second, total, gfirst, sems, out_sems = refs
    chunks = Chunks(first_hbm, second_hbm, first, second, sems)
    copies = experts_back_steps(
        x_ref[...],
        grad_ref[...],
        pre_ref,
        first,
        second,
        total,
        gfirst,
        None,
        (out_first, None),
        out_sems,
        chunks,
    )
    dx_ref[...] = total[...].astype(LOW)
    for one in copies:
        one.wait()


def experts_both_kernel(width, x_ref, cot_ref, *refs):
    first_hbm, second_hbm, y_ref, dx_ref, out_first, out_second = refs[:6]
    first, second, total, gfirst, gsecond, pre, sems, out_sems = refs[6:]
    chunks = Chunks(first_hbm, second_hbm, first, second, sems)
    x = x_ref[:, :width]
    experts_forward_steps(chunks, x, first, second, total, pre)
    y_low = total[...].astype(LOW)
    y_ref[...] = y_low
    cot = cot_ref[...].astype(WIDE)
    grad_gate = jnp.sum(y_low.astype(WIDE) * cot, axis=1, keepdims=True)
    high = grad_gate.astype(LOW).astype(WIDE)
    lane = lax.broadcasted_iota(jnp.int32, (x.shape[0], x_ref.shape[1] - width), 1)
    both = jnp.where(lane == 0, high, jnp.where(lane == 1, grad_gate - high, 0.0))
    dx_ref[:, width:] = both.astype(LOW)
    gate = x_ref[:, width : width + 1].astype(WIDE) + x_ref[:, width + 1 : width + 2].astype(WIDE)
    grad = (gate * cot).astype(LOW)
    copies = experts_back_steps(
        x, grad, pre, first, second, total, gfirst, gsecond, (out_first, out_second), out_sems, None
    )
    dx_ref[:, :width] = total[...].astype(LOW)
    for one in copies:
        one.wait()


def expert_call(kernel, arrays, first, second, shapes, with_grads, scratch):
    width, hidden = first.shape
    rows = arrays[0].shape[0]
    weights = [
        pltpu.VMEM((CHUNKS, width, hidden // CHUNKS), LOW),
        pltpu.VMEM((CHUNKS, hidden // CHUNKS, width), LOW),
    ]
    grads = [jax.ShapeDtypeStruct(one.shape, LOW) for one in (first, second)]
    sems = [pltpu.SemaphoreType.DMA((2, CHUNKS))]
    return pl.pallas_call(
        kernel,
        out_shape=(*shapes, *(grads if with_grads else [])),
        in_specs=[*in_vmem(len(arrays)), *any_specs(2)],
        out_specs=(*in_vmem(len(shapes)), *any_specs(2 if with_grads else 0)),
        scratch_shapes=[
            *weights,
            pltpu.VMEM((rows, width), WIDE),
            *(weights if with_grads else []),
            *scratch,
            *sems,
            *(sems if with_grads else []),
        ],
        compiler_params=pltpu.CompilerParams(vmem_limit_bytes=VMEM_BYTES),
    )(*arrays, first, second)


def pre_shape(rows, first):
    return (CHUNKS, rows, first.shape[1] // CHUNKS)


def run_experts(rows_in, first, second):
    shapes = [
        jax.ShapeDtypeStruct(rows_in.shape, LOW),
        jax.ShapeDtypeStruct(pre_shape(rows_in.shape[0], first), WIDE),
    ]
    return expert_call(experts_kernel, [rows_in], first, second, shapes, False, [])


def run_experts_second(pre, grad, second):
    hidden, width = second.shape
    return pl.pallas_call(
        experts_second_kernel,
        out_shape=jax.ShapeDtypeStruct(second.shape, LOW),
        in_specs=in_vmem(2),
        out_specs=any_specs(1)[0],
        scratch_shapes=[
            pltpu.VMEM((CHUNKS, hidden // CHUNKS, width), LOW),
            pltpu.SemaphoreType.DMA((CHUNKS,)),
        ],
        compiler_params=pltpu.CompilerParams(vmem_limit_bytes=VMEM_BYTES),
    )(pre, grad)


def run_experts_back(rows_in, grad, pre, first, second):
    width, hidden = first.shape
    weights = [
        pltpu.VMEM((CHUNKS, width, hidden // CHUNKS), LOW),
        pltpu.VMEM((CHUNKS, hidden // CHUNKS, width), LOW),
    ]
    return pl.pallas_call(
        experts_back_kernel,
        out_shape=[
            jax.ShapeDtypeStruct(rows_in.shape, LOW),
            jax.ShapeDtypeStruct(first.shape, LOW),
        ],
        in_specs=[*in_vmem(3), *any_specs(2)],
        out_specs=[*in_vmem(1), *any_specs(1)],
        scratch_shapes=[
            *weights,
            pltpu.VMEM(rows_in.shape, WIDE),
            weights[0],
            pltpu.SemaphoreType.DMA((2, CHUNKS)),
            pltpu.SemaphoreType.DMA((2, CHUNKS)),
        ],
        compiler_params=pltpu.CompilerParams(vmem_limit_bytes=VMEM_BYTES),
    )(rows_in, grad, pre, first, second)


def run_experts_both(rows_in, cot, first, second):
    kernel = functools.partial(experts_both_kernel, cot.shape[1])
    shapes = [jax.ShapeDtypeStruct(cot.shape, LOW), jax.ShapeDtypeStruct(rows_in.shape, LOW)]
    scratch = [pltpu.VMEM(pre_shape(cot.shape[0], first), WIDE)]
    return expert_call(kernel, [rows_in, cot], first, second, shapes, True, scratch)


def by_core(core, zero, one):
    return jnp.where(core == 0, zero, one)


def cut_kernel(words, first_ref, second_ref, first_mine, second_mine, first_sent, second_sent):
    first_mine[...] = first_ref[words[1]].astype(LOW)
    second_mine[...] = second_ref[words[1]].astype(LOW)
    first_sent[...] = first_ref[1 - words[1]].astype(LOW)
    second_sent[...] = second_ref[1 - words[1]].astype(LOW)


def cut_experts(words, first, second):
    shapes = [first.shape[1:], second.shape[1:]] * 2
    return pl.pallas_call(
        cut_kernel,
        out_shape=[jax.ShapeDtypeStruct(one, LOW) for one in shapes],
        in_specs=[pl.BlockSpec(memory_space=pltpu.SMEM), *in_vmem(2)],
        out_specs=in_vmem(4),
        compiler_params=pltpu.CompilerParams(vmem_limit_bytes=VMEM_BYTES),
    )(words, first, second)


def choose_kernel(count, words, *refs):
    zeros, ones, outs = refs[:count], refs[count : 2 * count], refs[2 * count :]

    def copy_all(sources):
        for source, out in zip(sources, outs):
            out[...] = source[...]

    @pl.when(words[1] == 0)
    def _():
        copy_all(zeros)

    @pl.when(words[1] != 0)
    def _():
        copy_all(ones)


def chosen_by_core(words, zeros, ones):
    count = len(zeros)
    return pl.pallas_call(
        functools.partial(choose_kernel, count),
        out_shape=[jax.ShapeDtypeStruct(one.shape, one.dtype) for one in zeros],
        in_specs=[pl.BlockSpec(memory_space=pltpu.SMEM), *in_vmem(2 * count)],
        out_specs=in_vmem(count),
        compiler_params=pltpu.CompilerParams(vmem_limit_bytes=VMEM_BYTES),
    )(words, *zeros, *ones)


def join_kernel(words, *refs):
    ones, twos, came, outs = refs[:2], refs[2:4], refs[4:6], refs[6:8]
    for at in range(2):
        outs[at][1 - words[1]] = came[at][...].astype(WIDE)

    @pl.when(words[1] == 0)
    def _():
        for at in range(2):
            outs[at][0] = ones[at][...].astype(WIDE)

    @pl.when(words[1] != 0)
    def _():
        for at in range(2):
            outs[at][1] = twos[at][...].astype(WIDE)


def join_experts(words, ones, twos, came):
    return pl.pallas_call(
        join_kernel,
        out_shape=[jax.ShapeDtypeStruct((2, *one.shape), WIDE) for one in ones],
        in_specs=[pl.BlockSpec(memory_space=pltpu.SMEM), *in_vmem(6)],
        out_specs=in_vmem(2),
        compiler_params=pltpu.CompilerParams(vmem_limit_bytes=VMEM_BYTES),
    )(words, *ones, *twos, *came)


def pack_kernel(words, small_ref, *refs):
    early_mine, early_sent, late_mine, late_sent = refs[4:]
    lead = small_ref.shape[1]
    early_mine[:, :lead] = small_ref[...]
    early_sent[:, :lead] = small_ref[...]
    for at, ref in enumerate(refs[:4]):
        half = ref.shape[1] // 2
        low, high = ref[:, :half], ref[:, half:]
        mine = by_core(words[1], low, high).astype(LOW)
        sent = by_core(words[1], high, low).astype(LOW)
        if at < 3:
            cols = slice(lead + at * half, lead + (at + 1) * half)
            early_mine[:, cols] = mine
            early_sent[:, cols] = sent
        else:
            late_mine[...] = mine
            late_sent[...] = sent


def pack_dense(words, small, weights):
    shard, width = weights[0].shape
    early, late = (shard, small.shape[1] + 3 * width // 2), (shard, width // 2)
    return pl.pallas_call(
        pack_kernel,
        out_shape=[jax.ShapeDtypeStruct(one, LOW) for one in (early, early, late, late)],
        in_specs=[pl.BlockSpec(memory_space=pltpu.SMEM), *in_vmem(5)],
        out_specs=in_vmem(4),
        compiler_params=pltpu.CompilerParams(vmem_limit_bytes=VMEM_BYTES),
    )(words, small, *weights)


def unpack_kernel(words, own_ref, came_ref, *outs):
    half = outs[0].shape[1] // 2
    for at, out in enumerate(outs[:4]):
        cols = slice(at * half, (at + 1) * half)
        own, came = own_ref[:, cols], came_ref[:, cols]
        out[:, :half] = by_core(words[1], own, came)
        out[:, half:] = by_core(words[1], came, own)
    outs[4][...] = own_ref[:, 4 * half :] + came_ref[:, 4 * half :]


def unpack_dense(words, own, came, width):
    shard = own.shape[0]
    shapes = [(shard, width)] * 4 + [(shard, own.shape[1] - 2 * width)]
    return pl.pallas_call(
        unpack_kernel,
        out_shape=[jax.ShapeDtypeStruct(one, WIDE) for one in shapes],
        in_specs=[pl.BlockSpec(memory_space=pltpu.SMEM), *in_vmem(2)],
        out_specs=in_vmem(5),
        compiler_params=pltpu.CompilerParams(vmem_limit_bytes=VMEM_BYTES),
    )(words, own, came)


def norm_back(grad_out, value, inverse, gain_row):
    scaled = grad_out * gain_row
    return inverse * (
        scaled - value * inverse * inverse * jnp.mean(scaled * value, axis=-1, keepdims=True)
    )


def sums_by_token_kernel(width, *refs):
    sent_ref, hot0, hot1, *more, out_ref = refs
    lanes = out_ref.shape[1] - width
    sent = sent_ref[:, :width]
    out_ref[:, :width] = dot_dims(hot0[...] + hot1[...], sent, 0, 0)
    lane = lax.broadcasted_iota(jnp.int32, (out_ref.shape[0], lanes), 1)
    parts = []
    for hot in (hot0, hot1):
        if more:
            returned_ref, grad_ref = more
            picked = dot_dims(hot[...], returned_ref[...], 0, 0)
            parts.append(jnp.sum(grad_ref[...].astype(WIDE) * picked, axis=1, keepdims=True))
        else:
            both = dot_dims(hot[...], sent_ref[:, width:], 0, 0)
            parts.append(both[:, :1] + both[:, 1:2])
    out_ref[:, width:] = jnp.where(lane == 0, parts[0], jnp.where(lane == 1, parts[1], 0.0))


def local_call(kernel, shapes, *arrays):
    def whole(one):
        if one.ndim == 1:
            return pl.BlockSpec(memory_space=pltpu.SMEM)
        return pl.BlockSpec(one.shape, lambda step: (0,) * one.ndim)

    return pl.pallas_call(
        kernel,
        grid=(1,),
        out_shape=shapes,
        in_specs=[whole(one) for one in arrays],
        out_specs=[whole(one) for one in shapes],
        compiler_params=pltpu.CompilerParams(vmem_limit_bytes=VMEM_BYTES),
    )(*arrays)


def column_sums(block, lanes, at):
    lane = lax.broadcasted_iota(jnp.int32, (block.shape[0], lanes), 1)
    return lax.dot_general(
        block,
        jnp.where(lane == at, 1.0, 0.0).astype(WIDE),
        (((0,), (0,)), ((), ())),
        precision=lax.Precision.HIGHEST,
        preferred_element_type=WIDE,
    )


def to_attention_kernel(words, *refs):
    mine_ref, other_ref, gates_ref, routes_ref, residual_ref, normed_ref, gain_ref = refs[:7]
    small_ref, out_w, grad_ref, dh_ref, attn_ref, branch_ref, grads_ref = refs[7:]
    width, lanes = residual_ref.shape[1], small_ref.shape[1]
    sums = mine_ref[...] + other_ref[...]
    grad_gates, gates = sums[:, width : width + 2], gates_ref[...]
    grad_chosen = gates * (grad_gates - jnp.sum(gates * grad_gates, axis=1, keepdims=True))
    routes = routes_ref[...]
    column = lax.broadcasted_iota(jnp.int32, (routes.shape[0], lanes), 1) - 2
    grad_logits = jnp.where(column == routes[:, :1], grad_chosen[:, :1], 0.0) + jnp.where(
        column == routes[:, 1:], grad_chosen[:, 1:2], 0.0
    )
    grad_logits = grad_logits.astype(LOW)
    grad_normed = sums[:, :width] + dot_dims(grad_logits, small_ref[...], 1, 1)
    residual = residual_ref[...]
    inverse = lax.rsqrt(jnp.mean(residual * residual, axis=1, keepdims=True) + EPS)
    grads_ref[...] = dot_dims(normed_ref[...], grad_logits, 0, 0) + column_sums(
        grad_normed * residual * inverse, lanes, 1
    )
    grad = grad_ref[...].astype(WIDE) + norm_back(grad_normed, residual, inverse, gain_ref[...])
    dh_ref[...] = grad
    low = grad.astype(LOW)
    half = branch_ref.shape[1]
    branch_ref[...] = by_core(words[1], low[:, :half], low[:, half:])
    heads = out_w[pl.ds(pl.multiple_of(words[1] * half, 16), half), :]
    attn_ref[...] = dot_dims(low, heads, 1, 1).astype(LOW)


def from_attention_kernel(count, *refs):
    query_ref, own_ref, *more = refs
    came, (weight_ref, qkv_ref, partial_ref) = more[:count], more[count:]
    half = query_ref.shape[1]
    total = own_ref[...]
    for one in came:
        total = total + one[...].astype(WIDE)
    qkv_ref[:, :half] = query_ref[...]
    qkv_ref[:, half:] = total.astype(LOW)
    partial_ref[...] = dot_dims(qkv_ref[...], weight_ref[...], 1, 1)


def to_input_kernel(mine_ref, other_ref, dh_ref, value_ref, gain_ref, small_ref, *refs):
    grad_normed = mine_ref[...] + other_ref[...]
    value = value_ref[...].astype(WIDE)
    inverse = lax.rsqrt(jnp.mean(value * value, axis=1, keepdims=True) + EPS)
    grad = dh_ref[...] + norm_back(grad_normed, value, inverse, gain_ref[...])
    grads_ref, out_ref, *slot_refs = refs[-2:] if len(refs) == 2 else refs[3:]
    grads_ref[...] = small_ref[...] + column_sums(
        grad_normed * value * inverse, grads_ref.shape[1], 0
    )
    out_ref[...] = grad
    if slot_refs:
        gates_ref, hot0, hot1 = refs[:3]
        low = grad.astype(LOW).astype(WIDE)
        rows = dot_wide(hot0[...], (gates_ref[:, :1] * low).astype(LOW))
        rows = rows + dot_wide(hot1[...], (gates_ref[:, 1:2] * low).astype(LOW))
        slot_refs[0][...] = rows.astype(LOW)


def body(
    inputs,
    cotangent,
    segments,
    buckets,
    routes,
    gain_attn,
    w_query,
    w_key,
    w_value,
    w_out,
    rel_bias,
    gain_moe,
    w_router,
    w_in,
    w_back,
):
    core = lax.axis_index("section")
    is_first = core == 0
    ctx_rank = lax.axis_index("ctx")
    ctx_count = lax.axis_size("ctx")
    exp_count = lax.axis_size("exp")
    held, rows, width = inputs.shape[0], inputs.shape[2], inputs.shape[3]
    groups = ctx_count // held
    parity = ctx_rank % held
    is_even = parity == 0
    group_rank = ctx_rank // held
    heads = rel_bias.shape[2]
    head_dim = width // heads
    half = width // 2
    half_heads = heads // 2
    local_exp = w_in.shape[1]
    experts = exp_count * local_exp
    capacity = 2 * rows // experts * 5 // 4
    bucket_count = rel_bias.shape[1] * ctx_count * exp_count
    shard = w_query.shape[1]
    rel_cols = rel_bias.shape[1] * heads // shard
    small_used = 2 + experts + rel_cols
    small_width = -(-small_used // 128) * 128
    extra = 128
    tokens = held * rows

    def regrouped(block):
        mine = lax.dynamic_index_in_dim(block, parity, 0, keepdims=False)
        sent = lax.dynamic_index_in_dim(block, 1 - parity, 0, keepdims=False)
        came = crossed(sent, 1)
        return jnp.where(is_even, jnp.stack([mine, came]), jnp.stack([came, mine]))

    def own_order(mine, other, axis):
        return jnp.where(
            is_first,
            jnp.concatenate([mine, other], axis=axis),
            jnp.concatenate([other, mine], axis=axis),
        )

    def both_cores(mine, axis=0):
        return own_order(mine, swapped(mine), axis)

    words = jnp.stack([ctx_rank, core]).astype(jnp.int32)
    small = jnp.concatenate(
        [
            gain_attn[0].astype(LOW)[:, None],
            gain_moe[0].astype(LOW)[:, None],
            w_router[0].astype(LOW),
            rel_bias[0].astype(LOW).reshape(shard, rel_cols),
            jnp.zeros((shard, small_width - small_used), LOW),
        ],
        axis=1,
    )

    def by_section(mine, other):
        return (jnp.where(is_first, mine, other), jnp.where(is_first, other, mine))

    first_mine, second_mine, first_sent, second_sent = cut_experts(words, w_in[0], w_back[0])
    own_shards, came_shards = [first_mine, second_mine], [swapped(first_sent), swapped(second_sent)]
    shards_one = chosen_by_core(words, own_shards, came_shards)
    early_mine, early_sent, late_mine, late_sent = pack_dense(
        tied(words, first_mine), small, [w[0] for w in (w_query, w_key, w_value, w_out)]
    )
    early_shards = by_section(early_mine, swapped(early_sent))
    late_shards = by_section(late_mine, swapped(late_sent))
    _, early_line = exp_line(early_shards[0])
    shards_two = chosen_by_core(words, came_shards, own_shards)

    def gathered(shards):
        return [lax.all_gather(one, "ctx", axis=0, tiled=True) for one in shards]

    seg_row = lax.dynamic_index_in_dim(segments[:, 0], parity, 0, keepdims=False)
    seg_blocks = seg_row.reshape(groups, held, rows)
    seg_keys = []
    for back in range(groups):
        seg = lax.dynamic_index_in_dim(
            seg_blocks, jnp.maximum(group_rank - back, 0), 0, keepdims=False
        )
        seg_keys.append(jnp.where(group_rank >= back, seg, -1))
    seg_q = seg_keys[0][:, :, None]
    seg_k = jnp.concatenate(seg_keys, axis=0)[:, None, :]

    back_order = jnp.flip(jnp.concatenate([jnp.broadcast_to(buckets[:1], (rows,)), buckets]))
    span = back_order.shape[0]
    by_distance = []
    for at in range(ctx_count):
        start = span - 2 * rows - at * rows
        by_distance.append(back_order[start : start + 2 * rows])
    bucket_vec = jnp.concatenate(by_distance)
    bucket_hot = (
        bucket_vec[:, None] == jnp.arange(bucket_count, dtype=jnp.int32)[None, :]
    ).astype(LOW)

    route_rows = regrouped(routes[:, 0])
    expert_ids = jnp.arange(experts, dtype=jnp.int32)
    flat_routes = route_rows.reshape(held, 2 * rows)
    member = (flat_routes[..., None] == expert_ids).astype(jnp.int32)
    slot_rank = jnp.sum((jnp.cumsum(member, axis=1) - member) * member, axis=-1)
    block_at = jnp.arange(held, dtype=jnp.int32)[:, None]
    slot_dest = ((flat_routes * held + block_at) * capacity + slot_rank).reshape(tokens, 2)
    exp_ids = jnp.arange(exp_count, dtype=jnp.int32)[:, None, None]
    in_block = block_at[None] * capacity + jnp.arange(capacity, dtype=jnp.int32)[None, None, :]
    slots = exp_count * held * capacity
    slot_ids = ((exp_ids * local_exp + core) * held * capacity + in_block).reshape(slots, 1)
    hots = [(slot_ids == slot_dest[None, :, c]).astype(LOW) for c in range(2)]
    to_token = hots[0] + hots[1]
    route_rows = route_rows.reshape(tokens, 2)
    small_ids = jnp.arange(small_width, dtype=jnp.int32)[None, :] - 2
    chosen_hot = [(route_rows[:, c : c + 1] == small_ids).astype(WIDE) for c in range(2)]

    def early_weights(early):
        tail = early[:, :small_width]
        rel = tail[:, 2 + experts : 2 + experts + rel_cols].reshape(bucket_count, heads)
        rel_mine = lax.dynamic_slice_in_dim(rel, core * half_heads, half_heads, 1)
        vec = dot_dims(rel_mine, bucket_hot, 0, 1)
        bias = bias_blocks(vec.reshape(half_heads, ctx_count, 1, 2 * rows), rows, ctx_count)
        return dict(
            qkv=early[:, small_width:],
            gain_a=tail[:, 0].astype(WIDE),
            gain_m=tail[:, 1].astype(WIDE),
            small=tail,
            bias=bias,
        )

    def late_weights(out_half):
        out_full = both_cores(out_half, 1)
        return dict(
            out=out_full, out_mine=lax.dynamic_slice_in_dim(out_full, core * half, half, 0)
        )

    def to_experts(rows_out):
        lanes = rows_out.shape[1]
        return lax.all_to_all(
            rows_out.reshape(exp_count, held * capacity, lanes),
            "exp",
            split_axis=0,
            concat_axis=0,
            tiled=True,
        ).reshape(slots, lanes)

    def in_two(wide):
        high = wide.astype(LOW)
        low = (wide - high.astype(WIDE)).astype(LOW)
        pad = jnp.zeros((wide.shape[0], extra - 2), LOW)
        return jnp.concatenate([high, low, pad], axis=1)

    def normed(value, gain_row):
        inverse = lax.rsqrt(jnp.mean(value * value, axis=-1, keepdims=True) + EPS)
        return (value * inverse * gain_row).astype(LOW), inverse

    def attention(normed_a, weights, arrived, arrived_after):
        qkv = dot_wide(normed_a, weights["qkv"]).astype(LOW)
        query, kv = qkv[:, :half], tied(qkv[:, half:], *arrived)
        kv_groups = [kv] + [shifted(kv, held * back) for back in range(1, groups)]
        attn_wide, attn_mine, log_total = attend(
            query, kv_groups, weights["bias"], seg_q, seg_k, rows, head_dim
        )
        attn_low = both_cores(tied(attn_mine, *arrived_after), 1)
        return dict(
            normed_a=normed_a,
            query=query,
            kv_groups=kv_groups,
            attn_wide=attn_wide,
            attn_low=attn_low,
            log_total=log_total,
        )

    def forward_to_experts(value, kept, weights, with_gates, arrived):
        residual = value + dot_wide(kept["attn_low"], weights["out"])
        normed_m, inv_m = normed(residual, weights["gain_m"])
        logits = dot_wide(normed_m, weights["small"])
        chosen = [jnp.sum(logits * hot_c, axis=-1, keepdims=True) for hot_c in chosen_hot]
        gates = jax.nn.softmax(jnp.concatenate(chosen, axis=1), axis=-1)
        sent = dot_wide(to_token, normed_m).astype(LOW)
        if with_gates:
            gate_rows = dot_wide(hots[0], in_two(gates[:, :1])) + dot_wide(
                hots[1], in_two(gates[:, 1:])
            )
            sent = jnp.concatenate([sent, gate_rows.astype(LOW)], axis=1)
        received = to_experts(tied(sent, *arrived))
        return dict(
            kept,
            value=value,
            residual=residual,
            inv_m=inv_m,
            normed_m=normed_m,
            gates=gates,
            received=received,
        )

    def combined(produced, kept):
        returned = to_experts(produced)
        picked = [dot_dims(hot_c, returned, 0, 0) for hot_c in hots]
        partial = kept["gates"][:, :1] * picked[0] + kept["gates"][:, 1:] * picked[1]
        return kept["residual"] + (partial + swapped(partial)), returned

    def wide_like(*shape):
        return jax.ShapeDtypeStruct(shape, WIDE)

    def low_like(*shape):
        return jax.ShapeDtypeStruct(shape, LOW)

    def backward_from_experts(grad_out, grad_sent, returned, weights, kept, below, arrived=()):
        more = [] if returned is None else [returned, grad_out]
        (partial,) = local_call(
            functools.partial(sums_by_token_kernel, width),
            [wide_like(tokens, width + extra)],
            grad_sent,
            *hots,
            *more,
        )
        grad_residual, grad_attn, branch_mine, small_part = local_call(
            to_attention_kernel,
            [
                wide_like(tokens, width),
                low_like(tokens, half),
                low_like(tokens, half),
                wide_like(width, small_width),
            ],
            words,
            partial,
            swapped(partial),
            kept["gates"],
            route_rows,
            kept["residual"],
            kept["normed_m"],
            weights["gain_m"][None],
            weights["small"],
            weights["out"],
            grad_out,
        )
        back = attend_back(
            kept["query"],
            kept["kv_groups"],
            weights["bias"],
            seg_q,
            seg_k,
            kept["log_total"],
            grad_attn,
            kept["attn_wide"],
            rows,
            head_dim,
        )
        grad_query, diag = tied(back[0], *arrived), back[-1]
        came = [shifted(back[1 + at], -held * at) for at in range(1, groups)]
        grad_qkv, partial = local_call(
            functools.partial(from_attention_kernel, groups - 1),
            [low_like(tokens, 3 * half), wide_like(tokens, width)],
            grad_query,
            back[1],
            *came,
            weights["qkv"],
        )
        slot_inputs = [] if below is None else [below, *hots]
        small_part, grad_value, *slot_rows = local_call(
            to_input_kernel,
            [wide_like(width, small_width), wide_like(tokens, width)]
            + ([] if below is None else [low_like(slots, width)]),
            partial,
            swapped(partial),
            grad_residual,
            kept["low"],
            weights["gain_a"][None],
            small_part,
            *slot_inputs,
        )
        grad_rel = lax.dot_general(
            bucket_hot.astype(WIDE),
            diag.reshape(half_heads, -1),
            (((0,), (1,)), ((), ())),
            precision=lax.Precision.HIGHEST,
            preferred_element_type=WIDE,
        )
        grad_rel = own_order(grad_rel, jnp.zeros_like(grad_rel), 1)
        rel_columns = jnp.pad(
            grad_rel.reshape(width, rel_cols),
            ((0, 0), (2 + experts, small_width - small_used)),
        )
        small_grads = (0.5 * small_part + rel_columns).astype(LOW)
        grads_of = (kept["normed_a"], grad_qkv, kept["attn_low"], branch_mine, small_grads)
        return grad_value, grads_of, grad_qkv, grad_attn, slot_rows

    def whole_dense_grads(normed_a, grad_qkv, attn_low, branch, small):
        qkv_w, out_w = dot_dims(normed_a, grad_qkv, 0, 0), dot_dims(attn_low, branch, 0, 0)
        return scattered_rows(
            jnp.concatenate([qkv_w.astype(LOW), out_w.astype(LOW), small], axis=1)
        )

    def summed_shards(grads):
        return [
            lax.psum_scatter(one, "ctx", scatter_dimension=0, tiled=True) for one in grads
        ]

    relayed = four_by_four()
    both = jnp.concatenate([early_shards[1], late_shards[1]], axis=1)
    if relayed:
        plane = plane_rows(both)
        planes = [plane] + sent_along_exp([plane] * 4)
        both = all_rows(planes, shard)
        early_line = tied(early_line, plane)
    else:
        planes = [both] * 4
        both = lax.all_gather(both, ("ctx", "exp"), axis=0, tiled=True)
    _, late_line = exp_line(tied(late_shards[0], early_line))
    early_one = tied(ctx_rows(early_line, []), late_line)
    dense_one = early_weights(early_one)
    value_low = regrouped(inputs[:, 0]).reshape(tokens, width)
    value = value_low.astype(WIDE)
    normed_a, inv_a = normed(value, dense_one["gain_a"])
    cot = regrouped(cotangent[:, 0]).reshape(tokens, width)
    experts_one = gathered(shards_one)
    kept_one = attention(normed_a, dense_one, [planes[1]], [planes[2]])
    kv_came = kept_one["kv_groups"][-1]
    dense_one = dict(dense_one, **late_weights(ctx_rows(late_line, [kv_came])))
    kept_one = forward_to_experts(value, kept_one, dense_one, False, [])
    kept_one["low"] = value_low
    experts_two = gathered([tied(one, kept_one["received"]) for one in shards_two])
    produced, pre_one = run_experts(kept_one["received"], *experts_one)
    out_one, returned_one = combined(tied(produced, planes[3]), kept_one)

    dense_two = dict(
        early_weights(both[:, : small_width + 3 * half]),
        **late_weights(both[:, small_width + 3 * half :]),
    )
    value_low = out_one.astype(LOW)
    value = value_low.astype(WIDE)
    normed_a, inv_a = normed(value, dense_two["gain_a"])
    kept_two = attention(normed_a, dense_two, [], [])
    cot_rows = to_experts(tied(dot_wide(to_token, cot).astype(LOW), out_one))
    kept_two = forward_to_experts(value, kept_two, dense_two, True, [cot_rows])
    kept_two["low"] = value_low
    produced, grad_rows, *grads_two = run_experts_both(
        kept_two["received"], cot_rows, *experts_two
    )
    grad_sent = to_experts(grad_rows)
    sums_two = summed_shards(grads_two)
    grad_two, grads_of_two, _, grad_attn, (slot_rows,) = backward_from_experts(
        cot, grad_sent, None, dense_two, kept_two, kept_one["gates"]
    )
    out_two, _ = combined(tied(produced, grad_attn), kept_two)

    grad_out = grad_two.astype(LOW)
    grad_rows = to_experts(slot_rows)
    if relayed:
        early_parts, late_parts = dense_grads(*grads_of_two)
        grad_rows = tied(grad_rows, *late_parts, *early_parts)
        early_hop = first_hop(early_parts, 2, 1)
    grad_rows, out_two = lax.optimization_barrier((grad_rows, out_two))
    second_grads = run_experts_second(pre_one, grad_rows, experts_one[1])
    sums_one = summed_shards([second_grads])
    grad_rows, first_grads = run_experts_back(
        kept_one["received"], grad_rows, tied(pre_one, second_grads), *experts_one
    )
    sums_one = summed_shards([first_grads]) + sums_one
    activations = regrouped(jnp.where(is_first, out_one, out_two).reshape(held, rows, width))
    grad_sent = to_experts(grad_rows)
    late_two = []
    if relayed:
        grad_sent, early_hop = lax.optimization_barrier((grad_sent, early_hop))
        late_two = sent_along_exp([tied(one, grad_sent) for one in late_parts])
    grad_one, grads_of_one, grad_qkv, _, _ = backward_from_experts(
        grad_out, grad_sent, returned_one, dense_one, kept_one, None, late_two
    )
    came = [swapped(one) for one in chosen_by_core(words, sums_two, sums_one)]
    if relayed:
        late_parts_two = late_parts
        early_parts, late_parts = dense_grads(*grads_of_one)
        late_two = [tied(one, late_parts[0]) for one in late_two]
        late_one = sent_along_exp(late_parts)
        early_one = over_ctx(early_parts)
        early_hop = [tied(one, late_one[0]) for one in early_hop]
        early_two = finished_along_exp(last_hop(early_hop, 1))
        dense_sum_one = jnp.concatenate(
            [finished_along_exp(early_one), finished_along_ctx(late_parts, late_one)], axis=1
        )
        dense_sum_two = jnp.concatenate(
            [early_two, finished_along_ctx(late_parts_two, late_two)], axis=1
        )
    else:
        dense_sum_two = whole_dense_grads(*grads_of_two)
        dense_sum_one = whole_dense_grads(*grads_of_one)

    grads_in = regrouped(jnp.where(is_first, grad_one, grad_two).reshape(held, rows, width))
    dense_own = jnp.where(is_first, dense_sum_one, dense_sum_two)
    dense_came = swapped(jnp.where(is_first, dense_sum_two, dense_sum_one))
    dense_own, *came = lax.optimization_barrier((dense_own, *came))
    query_out, key_out, value_out, outproj_out, tail = unpack_dense(
        words, dense_own, dense_came, width
    )
    rel_out = tail[:, 2 + experts : 2 + experts + rel_cols].reshape(rel_bias.shape)
    first_out, second_out = join_experts(words, sums_one, sums_two, came)
    out_shape = (1, held, 1, rows, width)
    return (
        activations.reshape(out_shape),
        grads_in.reshape(out_shape),
        tail[:, 0][None],
        query_out[None],
        key_out[None],
        value_out[None],
        outproj_out[None],
        rel_out,
        tail[:, 1][None],
        tail[:, 2 : 2 + experts][None],
        first_out[None],
        second_out[None],
    )


def solution(mesh):
    rows_spec = P("section", ("ctx", "exp"), None)
    gain_spec = P("section", ("ctx", "exp"))
    expert_spec = P("section", "exp", "ctx", None)
    token_spec = P(None, "exp", "ctx", None)
    state_spec = P("section", None, "exp", "ctx", None)
    in_specs = (
        token_spec,
        token_spec,
        P(None, "exp", None),
        P(),
        token_spec,
        gain_spec,
        *[rows_spec] * 5,
        gain_spec,
        rows_spec,
        *[expert_spec] * 2,
    )
    out_specs = (
        *[state_spec] * 2,
        gain_spec,
        *[rows_spec] * 5,
        gain_spec,
        rows_spec,
        *[expert_spec] * 2,
    )
    return jax.shard_map(body, mesh=mesh, in_specs=in_specs, out_specs=out_specs, check_vma=False)
```

```python
import functools

import jax
import jax.numpy as jnp
from jax import lax
from jax.experimental import pallas as pl
from jax.experimental.pallas import tpu as pltpu
from jax.sharding import PartitionSpec as P

EPS = 1e-06
NEG = -1e30
LOW = jnp.bfloat16
WIDE = jnp.float32
VMEM_BYTES = 48 * 1024 * 1024


def swapped(block):
    return lax.ppermute(block, "section", [(0, 1), (1, 0)])


def shifted(block, distance):
    size = lax.axis_size("ctx")
    route = [(i, i + distance) for i in range(size) if 0 <= i + distance < size]
    return lax.ppermute(block, "ctx", route)


def crossed(block, bits, axis="ctx"):
    return lax.ppermute(block, axis, [(i, i ^ bits) for i in range(lax.axis_size(axis))])


def tied(value, *others):
    return lax.optimization_barrier((value, *others))[0]


def place_kernel(moves, count, rank_ref, *refs):
    out_ref, sems = refs[count:]
    copies = []
    for number, (at, first, size, fixed, relation) in enumerate(moves):
        start = fixed + (rank_ref[0] ^ relation) * size
        target = out_ref.at[pl.ds(pl.multiple_of(start, 16), size)]
        copies.append(
            pltpu.make_async_copy(refs[at].at[pl.ds(first, size)], target, sems.at[number])
        )
        copies[-1].start()
    for one in copies:
        one.wait()


def placed(rank, pieces, moves, rows):
    return pl.pallas_call(
        functools.partial(place_kernel, moves, len(pieces)),
        out_shape=jax.ShapeDtypeStruct((rows, pieces[0].shape[1]), pieces[0].dtype),
        in_specs=[
            pl.BlockSpec(memory_space=pltpu.SMEM),
            *[pl.BlockSpec(memory_space=pl.ANY)] * len(pieces),
        ],
        out_specs=in_vmem(1)[0],
        scratch_shapes=[pltpu.SemaphoreType.DMA((len(moves),))],
        compiler_params=pltpu.CompilerParams(vmem_limit_bytes=VMEM_BYTES),
    )(rank.reshape(1), *pieces)


def four_by_four():
    return lax.axis_size("ctx") == 4 and lax.axis_size("exp") == 4


def exp_line(block):
    if not four_by_four():
        return [block] * 2, lax.all_gather(block, "exp", axis=0, tiled=True)
    shard = block.shape[0]
    along_exp = [block] + [crossed(block, k, "exp") for k in (1, 2, 3)]
    moves = [(k, 0, shard, 0, k) for k in range(4)]
    return along_exp, placed(lax.axis_index("exp"), along_exp, moves, 4 * shard)


def ctx_rows(line, before_relay):
    if not four_by_four():
        return lax.all_gather(line, "ctx", axis=0, tiled=True)
    from_x, from_y = crossed(line, 1), crossed(line, 2)
    along_ctx = [line, from_x, from_y, crossed(tied(from_x, *before_relay), 2)]
    size = line.shape[0]
    moves = [(k, 0, size, 0, k) for k in range(4)]
    return placed(lax.axis_index("ctx"), along_ctx, moves, 4 * size)


def plane_rows(block):
    from_x, from_y = crossed(block, 1), crossed(block, 2)
    along_ctx = [block, from_x, from_y, crossed(from_x, 2)]
    shard = block.shape[0]
    moves = [(k, 0, shard, 0, k) for k in range(4)]
    return placed(lax.axis_index("ctx"), along_ctx, moves, 4 * shard)


def all_rows(planes, shard):
    moves = [(k, at * shard, shard, at * 4 * shard, k) for k in range(4) for at in range(4)]
    return placed(lax.axis_index("exp"), planes, moves, 16 * shard)


def added(left, right):
    return left.astype(WIDE) + right.astype(WIDE)


def first_hop(parts, near, far):
    relayed = added(parts[far], crossed(parts[3], near)).astype(LOW)
    return added(parts[0], crossed(parts[near], near)), relayed


def last_hop(state, far):
    mine, relayed = state
    return mine + crossed(relayed, far).astype(WIDE)


def parts_for(blocks, axis, name):
    rank = lax.axis_index(name)
    return [lax.dynamic_index_in_dim(blocks, rank ^ k, axis, keepdims=False) for k in range(4)]


def over_exp(parts, came):
    total = parts[0].astype(WIDE)
    for one in came:
        total = total + one.astype(WIDE)
    return total


def over_ctx(parts):
    return last_hop(first_hop(parts, 2, 1), 1)


def sent_along_exp(parts):
    return [crossed(parts[k], k, "exp") for k in (1, 2, 3)]


def finished_along_ctx(parts, came):
    return over_ctx(parts_for(over_exp(parts, came).astype(LOW), 0, "ctx"))


def finished_along_exp(part):
    shard = part.shape[0] // 4
    parts = parts_for(part.astype(LOW).reshape(4, shard, part.shape[1]), 0, "exp")
    return over_exp(parts, sent_along_exp(parts))


def scattered_rows(block):
    block = lax.psum_scatter(block, "ctx", scatter_dimension=0, tiled=True)
    return lax.psum_scatter(block, "exp", scatter_dimension=0, tiled=True).astype(WIDE)


def dense_grads_kernel(ranks, normed_ref, grad_ref, attn_ref, branch_ref, small_ref, *refs):
    early_outs, late_outs, early, late = refs[:4], refs[4:8], refs[8], refs[9]
    cut, half = early.shape[1], branch_ref.shape[1]
    rest = grad_ref.shape[1] - cut
    early[...] = dot_dims(normed_ref[...], grad_ref[:, :cut], 0, 0).astype(LOW)
    late[:, :rest] = dot_dims(normed_ref[...], grad_ref[:, cut:], 0, 0).astype(LOW)
    late[:, rest : rest + half] = dot_dims(attn_ref[...], branch_ref[...], 0, 0).astype(LOW)
    late[:, rest + half :] = small_ref[...]
    shard = early.shape[0] // 16

    def rows_at(start):
        return pl.ds(pl.multiple_of(start, 16), shard)

    for k in range(4):
        at_exp = (ranks[1] ^ k) * shard
        for at in range(4):
            late_outs[k][at] = late[rows_at(at * 4 * shard + at_exp), :]
            start = (ranks[0] ^ k) * 4 * shard + at * shard
            early_outs[k][at * shard : (at + 1) * shard] = early[rows_at(start), :]


def dense_grads(normed_a, grad_qkv, attn_low, branch, small):
    width, half = normed_a.shape[1], branch.shape[1]
    shard = width // 16
    late_columns = half + half + small.shape[1]
    shapes = [(4 * shard, 2 * half)] * 4 + [(4, shard, late_columns)] * 4
    ranks = jnp.stack([lax.axis_index("ctx"), lax.axis_index("exp")]).astype(jnp.int32)
    out = pl.pallas_call(
        dense_grads_kernel,
        out_shape=[jax.ShapeDtypeStruct(one, LOW) for one in shapes],
        in_specs=[pl.BlockSpec(memory_space=pltpu.SMEM), *in_vmem(5)],
        out_specs=in_vmem(8),
        scratch_shapes=[pltpu.VMEM((width, 2 * half), LOW), pltpu.VMEM((width, late_columns), LOW)],
        compiler_params=pltpu.CompilerParams(vmem_limit_bytes=VMEM_BYTES),
    )(ranks, normed_a, grad_qkv, attn_low, branch, small)
    return out[:4], out[4:]


def in_vmem(count):
    return [pl.BlockSpec(memory_space=pltpu.VMEM)] * count


def dot_wide(left, right):
    return jnp.dot(left, right, preferred_element_type=WIDE)


def dot_dims(left, right, left_dim, right_dim):
    return lax.dot_general(
        left, right, (((left_dim,), (right_dim,)), ((), ())), preferred_element_type=WIDE
    )


def bias_kernel(rows, blocks, vec_ref, out_ref):
    for head in range(vec_ref.shape[0]):
        for at in range(blocks):
            wide = jnp.broadcast_to(vec_ref[head, at], (rows, 2 * rows))
            turned = pltpu.roll(wide, rows + 1, 1, stride=1, stride_axis=0)
            out_ref[
                head // 2, pl.ds((head % 2) * rows, rows), pl.ds(at * rows, rows)
            ] = turned[:, :rows]


def bias_blocks(vec, rows, blocks):
    heads = vec.shape[0]
    return pl.pallas_call(
        functools.partial(bias_kernel, rows, blocks),
        out_shape=jax.ShapeDtypeStruct((heads // 2, 2 * rows, blocks * rows), WIDE),
        in_specs=in_vmem(1),
        out_specs=in_vmem(1)[0],
        compiler_params=pltpu.CompilerParams(vmem_limit_bytes=VMEM_BYTES),
    )(vec)


def mask_rows(rows, at_q, key_blocks, seg_q, segk_ref):
    parts = []
    for back, at_k in enumerate(key_blocks):
        seg_k = segk_ref[at_k]
        good = (seg_k == 0) | (seg_k == seg_q)
        if back == 0:
            q_at = lax.broadcasted_iota(jnp.int32, (rows, rows), 0)
            k_at = lax.broadcasted_iota(jnp.int32, (rows, rows), 1)
            good = good & (q_at >= k_at)
        parts.append(jnp.where(good, 0.0, NEG).astype(WIDE))
    one = jnp.concatenate(parts, axis=1)
    return jnp.concatenate([one, one], axis=0)


def stacked_pair(block, half):
    lane = lax.broadcasted_iota(jnp.int32, block.shape, 1)
    zero = jnp.zeros_like(block)
    return jnp.concatenate(
        [jnp.where(lane < half, block, zero), jnp.where(lane >= half, block, zero)], axis=0
    )


def unstacked_pair(block, half):
    rows = block.shape[0] // 2
    lane = lax.broadcasted_iota(jnp.int32, (rows, block.shape[1]), 1)
    return jnp.where(lane < half, block[:rows], block[rows:])


def key_order(at_q, held, groups):
    near = [(0, at) for at in range(at_q, -1, -1)]
    return near + [(group, at) for group in range(1, groups) for at in range(held - 1, -1, -1)]


def attend_kernel(held, rows, groups, head_dim, *refs):
    q_ref, kv_refs = refs[0], refs[1 : 1 + groups]
    bias_ref, segq_ref, segk_ref, wide_ref, low_ref, log_ref = refs[1 + groups :]
    pairs = bias_ref.shape[0]
    lanes = 2 * head_dim
    width = pairs * lanes
    for at_q in range(held):
        order = key_order(at_q, held, groups)
        mask = mask_rows(rows, at_q, [g * held + at for g, at in order], segq_ref[at_q], segk_ref)
        here = pl.ds(at_q * rows, rows)
        for pair in range(pairs):
            cols = pl.ds(pair * lanes, lanes)
            vcols = pl.ds(width + pair * lanes, lanes)
            query = stacked_pair(q_ref[here, cols] * (head_dim**-0.5), head_dim)
            keys = jnp.concatenate(
                [kv_refs[g][pl.ds(at * rows, rows), cols] for g, at in order], axis=0
            )
            values = jnp.concatenate(
                [kv_refs[g][pl.ds(at * rows, rows), vcols] for g, at in order], axis=0
            )
            bias = bias_ref[pair, :, pl.ds(0, len(order) * rows)]
            scores = dot_dims(query, keys, 1, 1) + bias + mask
            top = jnp.max(scores, axis=1, keepdims=True)
            weights = jnp.exp(scores - top)
            total = jnp.sum(weights, axis=1, keepdims=True)
            out = dot_wide(weights.astype(LOW), values) / total
            log_ref[at_q * pairs + pair] = top + jnp.log(total)
            out = unstacked_pair(out, head_dim)
            wide_ref[here, cols] = out
            low_ref[here, cols] = out.astype(LOW)


def attend(query, kv_groups, bias, seg_q, seg_k, rows, head_dim):
    groups = len(kv_groups)
    held = query.shape[0] // rows
    pairs = bias.shape[0]
    return pl.pallas_call(
        functools.partial(attend_kernel, held, rows, groups, head_dim),
        out_shape=(
            jax.ShapeDtypeStruct(query.shape, WIDE),
            jax.ShapeDtypeStruct(query.shape, LOW),
            jax.ShapeDtypeStruct((held * pairs, 2 * rows, 1), WIDE),
        ),
        in_specs=in_vmem(4 + groups),
        out_specs=tuple(in_vmem(3)),
        compiler_params=pltpu.CompilerParams(vmem_limit_bytes=VMEM_BYTES),
    )(query, *kv_groups, bias, seg_q, seg_k)


def diagonal_sums(block):
    rows = block.shape[0]
    wide = jnp.concatenate([block, jnp.zeros_like(block)], axis=1)
    while rows > 8:
        rows //= 2
        wide = pltpu.roll(wide[:rows], rows, 1) + wide[rows:]
    row_at = lax.broadcasted_iota(jnp.int32, wide.shape, 0)
    for step in (4, 2, 1):
        wide = jnp.where(((7 - row_at) & step) != 0, pltpu.roll(wide, step, 1), wide)
    return jnp.sum(wide, axis=0, keepdims=True)


def attend_back_kernel(held, rows, groups, head_dim, *refs):
    q_ref, kv_refs = refs[0], refs[1 : 1 + groups]
    bias_ref, segq_ref, segk_ref, log_ref, grad_ref, wide_ref = refs[1 + groups : 7 + groups]
    dq_ref, dkv_refs = refs[7 + groups], refs[8 + groups : 8 + 2 * groups]
    diag_ref, acc_ref, dkv_acc = refs[8 + 2 * groups :]
    pairs = bias_ref.shape[0]
    lanes = 2 * head_dim
    width = pairs * lanes
    scale = head_dim**-0.5
    seen = set()

    def add_to(group, at, cols, block):
        here = pl.ds(at * rows, rows)
        if (group, at, cols.start) in seen:
            dkv_acc[group, here, cols] += block
        else:
            seen.add((group, at, cols.start))
            dkv_acc[group, here, cols] = block

    for at_q in range(held - 1, -1, -1):
        order = key_order(at_q, held, groups)
        mask = mask_rows(rows, at_q, [g * held + at for g, at in order], segq_ref[at_q], segk_ref)
        here = pl.ds(at_q * rows, rows)
        for pair in range(pairs):
            cols = pl.ds(pair * lanes, lanes)
            vcols = pl.ds(width + pair * lanes, lanes)
            query = stacked_pair(q_ref[here, cols] * scale, head_dim)
            grad = stacked_pair(grad_ref[here, cols], head_dim)
            wide = stacked_pair(wide_ref[here, cols], head_dim)
            delta = jnp.sum(grad.astype(WIDE) * wide, axis=1, keepdims=True)
            keys = jnp.concatenate(
                [kv_refs[g][pl.ds(at * rows, rows), cols] for g, at in order], axis=0
            )
            values = jnp.concatenate(
                [kv_refs[g][pl.ds(at * rows, rows), vcols] for g, at in order], axis=0
            )
            span = pl.ds(0, len(order) * rows)
            scores = dot_dims(query, keys, 1, 1) + bias_ref[pair, :, span] + mask
            probs = jnp.exp(scores - log_ref[at_q * pairs + pair])
            grad_probs = dot_dims(grad, values, 1, 1)
            grad_scores = (probs * (grad_probs - delta)).astype(LOW)
            grad_query = unstacked_pair(dot_wide(grad_scores, keys) * scale, head_dim)
            dq_ref[here, cols] = grad_query.astype(LOW)
            grad_keys = dot_dims(grad_scores, query, 0, 0)
            grad_values = dot_dims(probs.astype(LOW), grad, 0, 0)
            for back, (group, at) in enumerate(order):
                part = slice(back * rows, (back + 1) * rows)
                add_to(group, at, cols, grad_keys[part])
                add_to(group, at, vcols, grad_values[part])
            if at_q == held - 1:
                acc_ref[pair] = grad_scores.astype(WIDE)
            else:
                acc_ref[pair, :, span] += grad_scores.astype(WIDE)
    for group in range(groups):
        dkv_refs[group][...] = dkv_acc[group].astype(dkv_refs[group].dtype)
    for pair in range(pairs):
        for head in range(2):
            for at in range(held * groups):
                block = acc_ref[pair, pl.ds(head * rows, rows), pl.ds(at * rows, rows)]
                diag_ref[2 * pair + head, at] = diagonal_sums(block)


def attend_back(query, kv_groups, bias, seg_q, seg_k, log_total, grad, wide, rows, head_dim):
    groups = len(kv_groups)
    held = query.shape[0] // rows
    pairs = bias.shape[0]
    kv_shape = kv_groups[0].shape
    return pl.pallas_call(
        functools.partial(attend_back_kernel, held, rows, groups, head_dim),
        out_shape=(
            jax.ShapeDtypeStruct(query.shape, LOW),
            jax.ShapeDtypeStruct(kv_shape, WIDE),
            *[jax.ShapeDtypeStruct(kv_shape, LOW)] * (groups - 1),
            jax.ShapeDtypeStruct((2 * pairs, held * groups, 1, 2 * rows), WIDE),
        ),
        in_specs=in_vmem(7 + groups),
        out_specs=tuple(in_vmem(2 + groups)),
        scratch_shapes=[pltpu.VMEM(bias.shape, WIDE), pltpu.VMEM((groups, *kv_shape), WIDE)],
        compiler_params=pltpu.CompilerParams(vmem_limit_bytes=VMEM_BYTES),
    )(query, *kv_groups, bias, seg_q, seg_k, log_total, grad, wide)


GELU_A = 0.7978845608028654
GELU_B = 0.044715


def gelu_of(pre):
    return 0.5 * pre * (1.0 + jnp.tanh(GELU_A * (pre + GELU_B * pre * pre * pre)))


def gelu_and_slope(pre):
    square = pre * pre
    bent = jnp.tanh(GELU_A * pre * (1.0 + GELU_B * square))
    half_up = 0.5 * (1.0 + bent)
    slope = half_up + 0.5 * pre * (1.0 - bent * bent) * (
        GELU_A * (1.0 + 3.0 * GELU_B * square)
    )
    return pre * half_up, slope


def any_specs(count):
    return [pl.BlockSpec(memory_space=pl.ANY)] * count


CHUNKS = 4


class Chunks:
    def __init__(self, first_hbm, second_hbm, first, second, sems):
        hidden = second.shape[1]
        self.first_copies = [
            pltpu.make_async_copy(
                first_hbm.at[:, at * hidden : (at + 1) * hidden], first.at[at], sems.at[0, at]
            )
            for at in range(CHUNKS)
        ]
        self.second_copies = [
            pltpu.make_async_copy(
                second_hbm.at[at * hidden : (at + 1) * hidden], second.at[at], sems.at[1, at]
            )
            for at in range(CHUNKS)
        ]
        for first_copy, second_copy in zip(self.first_copies, self.second_copies):
            first_copy.start()
            second_copy.start()


def experts_forward_steps(chunks, x, first, second, total, pre_ref):
    for at in range(CHUNKS):
        chunks.first_copies[at].wait()
        pre = dot_wide(x, first[at])
        pre_ref[at] = pre
        act = gelu_of(pre).astype(LOW)
        chunks.second_copies[at].wait()
        part = dot_wide(act, second[at])
        total[...] = part if at == 0 else total[...] + part


def experts_back_steps(x, grad, pre_ref, first, second, total, gfirst, gsecond, outs, sems, chunks):
    out_first, out_second = outs
    hidden = second.shape[1]
    copies = []
    for at in range(CHUNKS):
        if chunks is not None:
            chunks.second_copies[at].wait()
            chunks.first_copies[at].wait()
        here = slice(at * hidden, (at + 1) * hidden)
        act, slope = gelu_and_slope(pre_ref[at])
        if gsecond is not None:
            gsecond[at] = dot_dims(act.astype(LOW), grad, 0, 0).astype(LOW)
            copies.append(
                pltpu.make_async_copy(gsecond.at[at], out_second.at[here], sems.at[1, at])
            )
            copies[-1].start()
        grad_act = dot_dims(grad, second[at], 1, 1)
        grad_pre = (grad_act * slope).astype(LOW)
        gfirst[at] = dot_dims(x, grad_pre, 0, 0).astype(LOW)
        copies.append(pltpu.make_async_copy(gfirst.at[at], out_first.at[:, here], sems.at[0, at]))
        copies[-1].start()
        part = dot_dims(grad_pre, first[at], 1, 1)
        total[...] = part if at == 0 else total[...] + part
    return copies


def experts_kernel(x_ref, first_hbm, second_hbm, y_ref, pre_ref, first, second, total, sems):
    chunks = Chunks(first_hbm, second_hbm, first, second, sems)
    experts_forward_steps(chunks, x_ref[...], first, second, total, pre_ref)
    y_ref[...] = total[...].astype(LOW)


def experts_second_kernel(pre_ref, grad_ref, out_ref, gsecond, sems):
    hidden = gsecond.shape[1]
    copies = []
    for at in range(CHUNKS):
        act = gelu_of(pre_ref[at]).astype(LOW)
        gsecond[at] = dot_dims(act, grad_ref[...], 0, 0).astype(LOW)
        target = out_ref.at[at * hidden : (at + 1) * hidden]
        copies.append(pltpu.make_async_copy(gsecond.at[at], target, sems.at[at]))
        copies[-1].start()
    for one in copies:
        one.wait()


def experts_back_kernel(x_ref, grad_ref, pre_ref, first_hbm, second_hbm, dx_ref, out_first, *refs):
    first, second, total, gfirst, sems, out_sems = refs
    chunks = Chunks(first_hbm, second_hbm, first, second, sems)
    copies = experts_back_steps(
        x_ref[...],
        grad_ref[...],
        pre_ref,
        first,
        second,
        total,
        gfirst,
        None,
        (out_first, None),
        out_sems,
        chunks,
    )
    dx_ref[...] = total[...].astype(LOW)
    for one in copies:
        one.wait()


def experts_both_kernel(width, x_ref, cot_ref, *refs):
    first_hbm, second_hbm, y_ref, dx_ref, out_first, out_second = refs[:6]
    first, second, total, gfirst, gsecond, pre, sems, out_sems = refs[6:]
    chunks = Chunks(first_hbm, second_hbm, first, second, sems)
    x = x_ref[:, :width]
    experts_forward_steps(chunks, x, first, second, total, pre)
    y_low = total[...].astype(LOW)
    y_ref[...] = y_low
    cot = cot_ref[...].astype(WIDE)
    grad_gate = jnp.sum(y_low.astype(WIDE) * cot, axis=1, keepdims=True)
    high = grad_gate.astype(LOW).astype(WIDE)
    lane = lax.broadcasted_iota(jnp.int32, (x.shape[0], x_ref.shape[1] - width), 1)
    both = jnp.where(lane == 0, high, jnp.where(lane == 1, grad_gate - high, 0.0))
    dx_ref[:, width:] = both.astype(LOW)
    gate = x_ref[:, width : width + 1].astype(WIDE) + x_ref[:, width + 1 : width + 2].astype(WIDE)
    grad = (gate * cot).astype(LOW)
    copies = experts_back_steps(
        x, grad, pre, first, second, total, gfirst, gsecond, (out_first, out_second), out_sems, None
    )
    dx_ref[:, :width] = total[...].astype(LOW)
    for one in copies:
        one.wait()


def expert_call(kernel, arrays, first, second, shapes, with_grads, scratch):
    width, hidden = first.shape
    rows = arrays[0].shape[0]
    weights = [
        pltpu.VMEM((CHUNKS, width, hidden // CHUNKS), LOW),
        pltpu.VMEM((CHUNKS, hidden // CHUNKS, width), LOW),
    ]
    grads = [jax.ShapeDtypeStruct(one.shape, LOW) for one in (first, second)]
    sems = [pltpu.SemaphoreType.DMA((2, CHUNKS))]
    return pl.pallas_call(
        kernel,
        out_shape=(*shapes, *(grads if with_grads else [])),
        in_specs=[*in_vmem(len(arrays)), *any_specs(2)],
        out_specs=(*in_vmem(len(shapes)), *any_specs(2 if with_grads else 0)),
        scratch_shapes=[
            *weights,
            pltpu.VMEM((rows, width), WIDE),
            *(weights if with_grads else []),
            *scratch,
            *sems,
            *(sems if with_grads else []),
        ],
        compiler_params=pltpu.CompilerParams(vmem_limit_bytes=VMEM_BYTES),
    )(*arrays, first, second)


def pre_shape(rows, first):
    return (CHUNKS, rows, first.shape[1] // CHUNKS)


def run_experts(rows_in, first, second):
    shapes = [
        jax.ShapeDtypeStruct(rows_in.shape, LOW),
        jax.ShapeDtypeStruct(pre_shape(rows_in.shape[0], first), WIDE),
    ]
    return expert_call(experts_kernel, [rows_in], first, second, shapes, False, [])


def run_experts_second(pre, grad, second):
    hidden, width = second.shape
    return pl.pallas_call(
        experts_second_kernel,
        out_shape=jax.ShapeDtypeStruct(second.shape, LOW),
        in_specs=in_vmem(2),
        out_specs=any_specs(1)[0],
        scratch_shapes=[
            pltpu.VMEM((CHUNKS, hidden // CHUNKS, width), LOW),
            pltpu.SemaphoreType.DMA((CHUNKS,)),
        ],
        compiler_params=pltpu.CompilerParams(vmem_limit_bytes=VMEM_BYTES),
    )(pre, grad)


def run_experts_back(rows_in, grad, pre, first, second):
    width, hidden = first.shape
    weights = [
        pltpu.VMEM((CHUNKS, width, hidden // CHUNKS), LOW),
        pltpu.VMEM((CHUNKS, hidden // CHUNKS, width), LOW),
    ]
    return pl.pallas_call(
        experts_back_kernel,
        out_shape=[
            jax.ShapeDtypeStruct(rows_in.shape, LOW),
            jax.ShapeDtypeStruct(first.shape, LOW),
        ],
        in_specs=[*in_vmem(3), *any_specs(2)],
        out_specs=[*in_vmem(1), *any_specs(1)],
        scratch_shapes=[
            *weights,
            pltpu.VMEM(rows_in.shape, WIDE),
            weights[0],
            pltpu.SemaphoreType.DMA((2, CHUNKS)),
            pltpu.SemaphoreType.DMA((2, CHUNKS)),
        ],
        compiler_params=pltpu.CompilerParams(vmem_limit_bytes=VMEM_BYTES),
    )(rows_in, grad, pre, first, second)


def run_experts_both(rows_in, cot, first, second):
    kernel = functools.partial(experts_both_kernel, cot.shape[1])
    shapes = [jax.ShapeDtypeStruct(cot.shape, LOW), jax.ShapeDtypeStruct(rows_in.shape, LOW)]
    scratch = [pltpu.VMEM(pre_shape(cot.shape[0], first), WIDE)]
    return expert_call(kernel, [rows_in, cot], first, second, shapes, True, scratch)


def by_core(core, zero, one):
    return jnp.where(core == 0, zero, one)


def cut_kernel(words, first_ref, second_ref, first_mine, second_mine, first_sent, second_sent):
    first_mine[...] = first_ref[words[1]].astype(LOW)
    second_mine[...] = second_ref[words[1]].astype(LOW)
    first_sent[...] = first_ref[1 - words[1]].astype(LOW)
    second_sent[...] = second_ref[1 - words[1]].astype(LOW)


def cut_experts(words, first, second):
    shapes = [first.shape[1:], second.shape[1:]] * 2
    return pl.pallas_call(
        cut_kernel,
        out_shape=[jax.ShapeDtypeStruct(one, LOW) for one in shapes],
        in_specs=[pl.BlockSpec(memory_space=pltpu.SMEM), *in_vmem(2)],
        out_specs=in_vmem(4),
        compiler_params=pltpu.CompilerParams(vmem_limit_bytes=VMEM_BYTES),
    )(words, first, second)


def choose_kernel(count, words, *refs):
    zeros, ones, outs = refs[:count], refs[count : 2 * count], refs[2 * count :]

    def copy_all(sources):
        for source, out in zip(sources, outs):
            out[...] = source[...]

    @pl.when(words[1] == 0)
    def _():
        copy_all(zeros)

    @pl.when(words[1] != 0)
    def _():
        copy_all(ones)


def chosen_by_core(words, zeros, ones):
    count = len(zeros)
    return pl.pallas_call(
        functools.partial(choose_kernel, count),
        out_shape=[jax.ShapeDtypeStruct(one.shape, one.dtype) for one in zeros],
        in_specs=[pl.BlockSpec(memory_space=pltpu.SMEM), *in_vmem(2 * count)],
        out_specs=in_vmem(count),
        compiler_params=pltpu.CompilerParams(vmem_limit_bytes=VMEM_BYTES),
    )(words, *zeros, *ones)


def join_kernel(words, *refs):
    ones, twos, came, outs = refs[:2], refs[2:4], refs[4:6], refs[6:8]
    for at in range(2):
        outs[at][1 - words[1]] = came[at][...].astype(WIDE)

    @pl.when(words[1] == 0)
    def _():
        for at in range(2):
            outs[at][0] = ones[at][...].astype(WIDE)

    @pl.when(words[1] != 0)
    def _():
        for at in range(2):
            outs[at][1] = twos[at][...].astype(WIDE)


def join_experts(words, ones, twos, came):
    return pl.pallas_call(
        join_kernel,
        out_shape=[jax.ShapeDtypeStruct((2, *one.shape), WIDE) for one in ones],
        in_specs=[pl.BlockSpec(memory_space=pltpu.SMEM), *in_vmem(6)],
        out_specs=in_vmem(2),
        compiler_params=pltpu.CompilerParams(vmem_limit_bytes=VMEM_BYTES),
    )(words, *ones, *twos, *came)


def pack_kernel(words, small_ref, *refs):
    early_mine, early_sent, late_mine, late_sent = refs[4:]
    lead = small_ref.shape[1]
    early_mine[:, :lead] = small_ref[...]
    early_sent[:, :lead] = small_ref[...]
    for at, ref in enumerate(refs[:4]):
        half = ref.shape[1] // 2
        low, high = ref[:, :half], ref[:, half:]
        mine = by_core(words[1], low, high).astype(LOW)
        sent = by_core(words[1], high, low).astype(LOW)
        if at < 3:
            cols = slice(lead + at * half, lead + (at + 1) * half)
            early_mine[:, cols] = mine
            early_sent[:, cols] = sent
        else:
            late_mine[...] = mine
            late_sent[...] = sent


def pack_dense(words, small, weights):
    shard, width = weights[0].shape
    early, late = (shard, small.shape[1] + 3 * width // 2), (shard, width // 2)
    return pl.pallas_call(
        pack_kernel,
        out_shape=[jax.ShapeDtypeStruct(one, LOW) for one in (early, early, late, late)],
        in_specs=[pl.BlockSpec(memory_space=pltpu.SMEM), *in_vmem(5)],
        out_specs=in_vmem(4),
        compiler_params=pltpu.CompilerParams(vmem_limit_bytes=VMEM_BYTES),
    )(words, small, *weights)


def unpack_kernel(words, own_ref, came_ref, *outs):
    half = outs[0].shape[1] // 2
    for at, out in enumerate(outs[:4]):
        cols = slice(at * half, (at + 1) * half)
        own, came = own_ref[:, cols], came_ref[:, cols]
        out[:, :half] = by_core(words[1], own, came)
        out[:, half:] = by_core(words[1], came, own)
    outs[4][...] = own_ref[:, 4 * half :] + came_ref[:, 4 * half :]


def unpack_dense(words, own, came, width):
    shard = own.shape[0]
    shapes = [(shard, width)] * 4 + [(shard, own.shape[1] - 2 * width)]
    return pl.pallas_call(
        unpack_kernel,
        out_shape=[jax.ShapeDtypeStruct(one, WIDE) for one in shapes],
        in_specs=[pl.BlockSpec(memory_space=pltpu.SMEM), *in_vmem(2)],
        out_specs=in_vmem(5),
        compiler_params=pltpu.CompilerParams(vmem_limit_bytes=VMEM_BYTES),
    )(words, own, came)


def norm_back(grad_out, value, inverse, gain_row):
    scaled = grad_out * gain_row
    return inverse * (
        scaled - value * inverse * inverse * jnp.mean(scaled * value, axis=-1, keepdims=True)
    )


def sums_by_token_kernel(width, *refs):
    sent_ref, hot0, hot1, *more, out_ref = refs
    lanes = out_ref.shape[1] - width
    sent = sent_ref[:, :width]
    out_ref[:, :width] = dot_dims(hot0[...] + hot1[...], sent, 0, 0)
    lane = lax.broadcasted_iota(jnp.int32, (out_ref.shape[0], lanes), 1)
    parts = []
    for hot in (hot0, hot1):
        if more:
            returned_ref, grad_ref = more
            picked = dot_dims(hot[...], returned_ref[...], 0, 0)
            parts.append(jnp.sum(grad_ref[...].astype(WIDE) * picked, axis=1, keepdims=True))
        else:
            both = dot_dims(hot[...], sent_ref[:, width:], 0, 0)
            parts.append(both[:, :1] + both[:, 1:2])
    out_ref[:, width:] = jnp.where(lane == 0, parts[0], jnp.where(lane == 1, parts[1], 0.0))


def local_call(kernel, shapes, *arrays):
    def whole(one):
        if one.ndim == 1:
            return pl.BlockSpec(memory_space=pltpu.SMEM)
        return pl.BlockSpec(one.shape, lambda step: (0,) * one.ndim)

    return pl.pallas_call(
        kernel,
        grid=(1,),
        out_shape=shapes,
        in_specs=[whole(one) for one in arrays],
        out_specs=[whole(one) for one in shapes],
        compiler_params=pltpu.CompilerParams(vmem_limit_bytes=VMEM_BYTES),
    )(*arrays)


def column_sums(block, lanes, at):
    lane = lax.broadcasted_iota(jnp.int32, (block.shape[0], lanes), 1)
    return lax.dot_general(
        block,
        jnp.where(lane == at, 1.0, 0.0).astype(WIDE),
        (((0,), (0,)), ((), ())),
        precision=lax.Precision.HIGHEST,
        preferred_element_type=WIDE,
    )


def to_attention_kernel(words, *refs):
    mine_ref, other_ref, gates_ref, routes_ref, residual_ref, normed_ref, gain_ref = refs[:7]
    small_ref, out_w, grad_ref, dh_ref, attn_ref, branch_ref, grads_ref = refs[7:]
    width, lanes = residual_ref.shape[1], small_ref.shape[1]
    sums = mine_ref[...] + other_ref[...]
    grad_gates, gates = sums[:, width : width + 2], gates_ref[...]
    grad_chosen = gates * (grad_gates - jnp.sum(gates * grad_gates, axis=1, keepdims=True))
    routes = routes_ref[...]
    column = lax.broadcasted_iota(jnp.int32, (routes.shape[0], lanes), 1) - 2
    grad_logits = jnp.where(column == routes[:, :1], grad_chosen[:, :1], 0.0) + jnp.where(
        column == routes[:, 1:], grad_chosen[:, 1:2], 0.0
    )
    grad_logits = grad_logits.astype(LOW)
    grad_normed = sums[:, :width] + dot_dims(grad_logits, small_ref[...], 1, 1)
    residual = residual_ref[...]
    inverse = lax.rsqrt(jnp.mean(residual * residual, axis=1, keepdims=True) + EPS)
    grads_ref[...] = dot_dims(normed_ref[...], grad_logits, 0, 0) + column_sums(
        grad_normed * residual * inverse, lanes, 1
    )
    grad = grad_ref[...].astype(WIDE) + norm_back(grad_normed, residual, inverse, gain_ref[...])
    dh_ref[...] = grad
    low = grad.astype(LOW)
    half = branch_ref.shape[1]
    branch_ref[...] = by_core(words[1], low[:, :half], low[:, half:])
    heads = out_w[pl.ds(pl.multiple_of(words[1] * half, 16), half), :]
    attn_ref[...] = dot_dims(low, heads, 1, 1).astype(LOW)


def from_attention_kernel(count, *refs):
    query_ref, own_ref, *more = refs
    came, (weight_ref, qkv_ref, partial_ref) = more[:count], more[count:]
    half = query_ref.shape[1]
    total = own_ref[...]
    for one in came:
        total = total + one[...].astype(WIDE)
    qkv_ref[:, :half] = query_ref[...]
    qkv_ref[:, half:] = total.astype(LOW)
    partial_ref[...] = dot_dims(qkv_ref[...], weight_ref[...], 1, 1)


def to_input_kernel(mine_ref, other_ref, dh_ref, value_ref, gain_ref, small_ref, *refs):
    grad_normed = mine_ref[...] + other_ref[...]
    value = value_ref[...].astype(WIDE)
    inverse = lax.rsqrt(jnp.mean(value * value, axis=1, keepdims=True) + EPS)
    grad = dh_ref[...] + norm_back(grad_normed, value, inverse, gain_ref[...])
    grads_ref, out_ref, *slot_refs = refs[-2:] if len(refs) == 2 else refs[3:]
    grads_ref[...] = small_ref[...] + column_sums(
        grad_normed * value * inverse, grads_ref.shape[1], 0
    )
    out_ref[...] = grad
    if slot_refs:
        gates_ref, hot0, hot1 = refs[:3]
        low = grad.astype(LOW).astype(WIDE)
        rows = dot_wide(hot0[...], (gates_ref[:, :1] * low).astype(LOW))
        rows = rows + dot_wide(hot1[...], (gates_ref[:, 1:2] * low).astype(LOW))
        slot_refs[0][...] = rows.astype(LOW)


def body(
    inputs,
    cotangent,
    segments,
    buckets,
    routes,
    gain_attn,
    w_query,
    w_key,
    w_value,
    w_out,
    rel_bias,
    gain_moe,
    w_router,
    w_in,
    w_back,
):
    core = lax.axis_index("section")
    is_first = core == 0
    ctx_rank = lax.axis_index("ctx")
    ctx_count = lax.axis_size("ctx")
    exp_count = lax.axis_size("exp")
    held, rows, width = inputs.shape[0], inputs.shape[2], inputs.shape[3]
    groups = ctx_count // held
    parity = ctx_rank % held
    is_even = parity == 0
    group_rank = ctx_rank // held
    heads = rel_bias.shape[2]
    head_dim = width // heads
    half = width // 2
    half_heads = heads // 2
    local_exp = w_in.shape[1]
    experts = exp_count * local_exp
    capacity = 2 * rows // experts * 5 // 4
    bucket_count = rel_bias.shape[1] * ctx_count * exp_count
    shard = w_query.shape[1]
    rel_cols = rel_bias.shape[1] * heads // shard
    small_used = 2 + experts + rel_cols
    small_width = -(-small_used // 128) * 128
    extra = 128
    tokens = held * rows

    def regrouped(block):
        mine = lax.dynamic_index_in_dim(block, parity, 0, keepdims=False)
        sent = lax.dynamic_index_in_dim(block, 1 - parity, 0, keepdims=False)
        if block.dtype == WIDE:
            sent = sent.astype(LOW)
        came = crossed(sent, 1).astype(block.dtype)
        return jnp.where(is_even, jnp.stack([mine, came]), jnp.stack([came, mine]))

    def own_order(mine, other, axis):
        return jnp.where(
            is_first,
            jnp.concatenate([mine, other], axis=axis),
            jnp.concatenate([other, mine], axis=axis),
        )

    def both_cores(mine, axis=0):
        return own_order(mine, swapped(mine), axis)

    words = jnp.stack([ctx_rank, core]).astype(jnp.int32)
    small = jnp.concatenate(
        [
            gain_attn[0].astype(LOW)[:, None],
            gain_moe[0].astype(LOW)[:, None],
            w_router[0].astype(LOW),
            rel_bias[0].astype(LOW).reshape(shard, rel_cols),
            jnp.zeros((shard, small_width - small_used), LOW),
        ],
        axis=1,
    )

    def by_section(mine, other):
        return (jnp.where(is_first, mine, other), jnp.where(is_first, other, mine))

    first_mine, second_mine, first_sent, second_sent = cut_experts(words, w_in[0], w_back[0])
    own_shards, came_shards = [first_mine, second_mine], [swapped(first_sent), swapped(second_sent)]
    shards_one = chosen_by_core(words, own_shards, came_shards)
    early_mine, early_sent, late_mine, late_sent = pack_dense(
        tied(words, first_mine), small, [w[0] for w in (w_query, w_key, w_value, w_out)]
    )
    early_shards = by_section(early_mine, swapped(early_sent))
    late_shards = by_section(late_mine, swapped(late_sent))
    _, early_line = exp_line(early_shards[0])
    shards_two = chosen_by_core(words, came_shards, own_shards)

    def gathered(shards):
        return [lax.all_gather(one, "ctx", axis=0, tiled=True) for one in shards]

    seg_row = lax.dynamic_index_in_dim(segments[:, 0], parity, 0, keepdims=False)
    seg_blocks = seg_row.reshape(groups, held, rows)
    seg_keys = []
    for back in range(groups):
        seg = lax.dynamic_index_in_dim(
            seg_blocks, jnp.maximum(group_rank - back, 0), 0, keepdims=False
        )
        seg_keys.append(jnp.where(group_rank >= back, seg, -1))
    seg_q = seg_keys[0][:, :, None]
    seg_k = jnp.concatenate(seg_keys, axis=0)[:, None, :]

    back_order = jnp.flip(jnp.concatenate([jnp.broadcast_to(buckets[:1], (rows,)), buckets]))
    span = back_order.shape[0]
    by_distance = []
    for at in range(ctx_count):
        start = span - 2 * rows - at * rows
        by_distance.append(back_order[start : start + 2 * rows])
    bucket_vec = jnp.concatenate(by_distance)
    bucket_hot = (
        bucket_vec[:, None] == jnp.arange(bucket_count, dtype=jnp.int32)[None, :]
    ).astype(LOW)

    route_rows = regrouped(routes[:, 0])
    expert_ids = jnp.arange(experts, dtype=jnp.int32)
    flat_routes = route_rows.reshape(held, 2 * rows)
    member = (flat_routes[..., None] == expert_ids).astype(jnp.int32)
    slot_rank = jnp.sum((jnp.cumsum(member, axis=1) - member) * member, axis=-1)
    block_at = jnp.arange(held, dtype=jnp.int32)[:, None]
    slot_dest = ((flat_routes * held + block_at) * capacity + slot_rank).reshape(tokens, 2)
    exp_ids = jnp.arange(exp_count, dtype=jnp.int32)[:, None, None]
    in_block = block_at[None] * capacity + jnp.arange(capacity, dtype=jnp.int32)[None, None, :]
    slots = exp_count * held * capacity
    slot_ids = ((exp_ids * local_exp + core) * held * capacity + in_block).reshape(slots, 1)
    hots = [(slot_ids == slot_dest[None, :, c]).astype(LOW) for c in range(2)]
    to_token = hots[0] + hots[1]
    route_rows = route_rows.reshape(tokens, 2)
    small_ids = jnp.arange(small_width, dtype=jnp.int32)[None, :] - 2
    chosen_hot = [(route_rows[:, c : c + 1] == small_ids).astype(WIDE) for c in range(2)]

    def early_weights(early):
        tail = early[:, :small_width]
        rel = tail[:, 2 + experts : 2 + experts + rel_cols].reshape(bucket_count, heads)
        rel_mine = lax.dynamic_slice_in_dim(rel, core * half_heads, half_heads, 1)
        vec = dot_dims(rel_mine, bucket_hot, 0, 1)
        bias = bias_blocks(vec.reshape(half_heads, ctx_count, 1, 2 * rows), rows, ctx_count)
        return dict(
            qkv=early[:, small_width:],
            gain_a=tail[:, 0].astype(WIDE),
            gain_m=tail[:, 1].astype(WIDE),
            small=tail,
            bias=bias,
        )

    def late_weights(out_half):
        out_full = both_cores(out_half, 1)
        return dict(
            out=out_full, out_mine=lax.dynamic_slice_in_dim(out_full, core * half, half, 0)
        )

    def to_experts(rows_out):
        lanes = rows_out.shape[1]
        return lax.all_to_all(
            rows_out.reshape(exp_count, held * capacity, lanes),
            "exp",
            split_axis=0,
            concat_axis=0,
            tiled=True,
        ).reshape(slots, lanes)

    def in_two(wide):
        high = wide.astype(LOW)
        low = (wide - high.astype(WIDE)).astype(LOW)
        pad = jnp.zeros((wide.shape[0], extra - 2), LOW)
        return jnp.concatenate([high, low, pad], axis=1)

    def normed(value, gain_row):
        inverse = lax.rsqrt(jnp.mean(value * value, axis=-1, keepdims=True) + EPS)
        return (value * inverse * gain_row).astype(LOW), inverse

    def attention(normed_a, weights, arrived, arrived_after):
        qkv = dot_wide(normed_a, weights["qkv"]).astype(LOW)
        query, kv = qkv[:, :half], tied(qkv[:, half:], *arrived)
        kv_groups = [kv] + [shifted(kv, held * back) for back in range(1, groups)]
        attn_wide, attn_mine, log_total = attend(
            query, kv_groups, weights["bias"], seg_q, seg_k, rows, head_dim
        )
        attn_low = both_cores(tied(attn_mine, *arrived_after), 1)
        return dict(
            normed_a=normed_a,
            query=query,
            kv_groups=kv_groups,
            attn_wide=attn_wide,
            attn_low=attn_low,
            log_total=log_total,
        )

    def forward_to_experts(value, kept, weights, with_gates, arrived):
        residual = value + dot_wide(kept["attn_low"], weights["out"])
        normed_m, inv_m = normed(residual, weights["gain_m"])
        logits = dot_wide(normed_m, weights["small"])
        chosen = [jnp.sum(logits * hot_c, axis=-1, keepdims=True) for hot_c in chosen_hot]
        gates = jax.nn.softmax(jnp.concatenate(chosen, axis=1), axis=-1)
        sent = dot_wide(to_token, normed_m).astype(LOW)
        if with_gates:
            gate_rows = dot_wide(hots[0], in_two(gates[:, :1])) + dot_wide(
                hots[1], in_two(gates[:, 1:])
            )
            sent = jnp.concatenate([sent, gate_rows.astype(LOW)], axis=1)
        received = to_experts(tied(sent, *arrived))
        return dict(
            kept,
            value=value,
            residual=residual,
            inv_m=inv_m,
            normed_m=normed_m,
            gates=gates,
            received=received,
        )

    def combined(produced, kept):
        returned = to_experts(produced)
        picked = [dot_dims(hot_c, returned, 0, 0) for hot_c in hots]
        partial = kept["gates"][:, :1] * picked[0] + kept["gates"][:, 1:] * picked[1]
        return kept["residual"] + (partial + swapped(partial)), returned

    def wide_like(*shape):
        return jax.ShapeDtypeStruct(shape, WIDE)

    def low_like(*shape):
        return jax.ShapeDtypeStruct(shape, LOW)

    def backward_from_experts(grad_out, grad_sent, returned, weights, kept, below, arrived=()):
        more = [] if returned is None else [returned, grad_out]
        (partial,) = local_call(
            functools.partial(sums_by_token_kernel, width),
            [wide_like(tokens, width + extra)],
            grad_sent,
            *hots,
            *more,
        )
        grad_residual, grad_attn, branch_mine, small_part = local_call(
            to_attention_kernel,
            [
                wide_like(tokens, width),
                low_like(tokens, half),
                low_like(tokens, half),
                wide_like(width, small_width),
            ],
            words,
            partial,
            swapped(partial),
            kept["gates"],
            route_rows,
            kept["residual"],
            kept["normed_m"],
            weights["gain_m"][None],
            weights["small"],
            weights["out"],
            grad_out,
        )
        back = attend_back(
            kept["query"],
            kept["kv_groups"],
            weights["bias"],
            seg_q,
            seg_k,
            kept["log_total"],
            grad_attn,
            kept["attn_wide"],
            rows,
            head_dim,
        )
        grad_query, diag = tied(back[0], *arrived), back[-1]
        came = [shifted(back[1 + at], -held * at) for at in range(1, groups)]
        grad_qkv, partial = local_call(
            functools.partial(from_attention_kernel, groups - 1),
            [low_like(tokens, 3 * half), wide_like(tokens, width)],
            grad_query,
            back[1],
            *came,
            weights["qkv"],
        )
        slot_inputs = [] if below is None else [below, *hots]
        small_part, grad_value, *slot_rows = local_call(
            to_input_kernel,
            [wide_like(width, small_width), wide_like(tokens, width)]
            + ([] if below is None else [low_like(slots, width)]),
            partial,
            swapped(partial),
            grad_residual,
            kept["low"],
            weights["gain_a"][None],
            small_part,
            *slot_inputs,
        )
        grad_rel = lax.dot_general(
            bucket_hot.astype(WIDE),
            diag.reshape(half_heads, -1),
            (((0,), (1,)), ((), ())),
            precision=lax.Precision.HIGHEST,
            preferred_element_type=WIDE,
        )
        grad_rel = own_order(grad_rel, jnp.zeros_like(grad_rel), 1)
        rel_columns = jnp.pad(
            grad_rel.reshape(width, rel_cols),
            ((0, 0), (2 + experts, small_width - small_used)),
        )
        small_grads = (0.5 * small_part + rel_columns).astype(LOW)
        grads_of = (kept["normed_a"], grad_qkv, kept["attn_low"], branch_mine, small_grads)
        return grad_value, grads_of, grad_qkv, grad_attn, slot_rows

    def whole_dense_grads(normed_a, grad_qkv, attn_low, branch, small):
        qkv_w, out_w = dot_dims(normed_a, grad_qkv, 0, 0), dot_dims(attn_low, branch, 0, 0)
        return scattered_rows(
            jnp.concatenate([qkv_w.astype(LOW), out_w.astype(LOW), small], axis=1)
        )

    def summed_shards(grads):
        return [
            lax.psum_scatter(one, "ctx", scatter_dimension=0, tiled=True) for one in grads
        ]

    relayed = four_by_four()
    both = jnp.concatenate([early_shards[1], late_shards[1]], axis=1)
    if relayed:
        plane = plane_rows(both)
        planes = [plane] + sent_along_exp([plane] * 4)
        both = all_rows(planes, shard)
        early_line = tied(early_line, plane)
    else:
        planes = [both] * 4
        both = lax.all_gather(both, ("ctx", "exp"), axis=0, tiled=True)
    _, late_line = exp_line(tied(late_shards[0], early_line))
    early_one = tied(ctx_rows(early_line, []), late_line)
    dense_one = early_weights(early_one)
    value_low = regrouped(inputs[:, 0]).reshape(tokens, width)
    value = value_low.astype(WIDE)
    normed_a, inv_a = normed(value, dense_one["gain_a"])
    cot = regrouped(cotangent[:, 0]).reshape(tokens, width)
    experts_one = gathered(shards_one)
    kept_one = attention(normed_a, dense_one, [planes[1]], [planes[2]])
    kv_came = kept_one["kv_groups"][-1]
    dense_one = dict(dense_one, **late_weights(ctx_rows(late_line, [kv_came])))
    kept_one = forward_to_experts(value, kept_one, dense_one, False, [])
    kept_one["low"] = value_low
    experts_two = gathered([tied(one, kept_one["received"]) for one in shards_two])
    produced, pre_one = run_experts(kept_one["received"], *experts_one)
    out_one, returned_one = combined(tied(produced, planes[3]), kept_one)

    dense_two = dict(
        early_weights(both[:, : small_width + 3 * half]),
        **late_weights(both[:, small_width + 3 * half :]),
    )
    value_low = out_one.astype(LOW)
    value = value_low.astype(WIDE)
    normed_a, inv_a = normed(value, dense_two["gain_a"])
    kept_two = attention(normed_a, dense_two, [], [])
    cot_rows = to_experts(tied(dot_wide(to_token, cot).astype(LOW), out_one))
    kept_two = forward_to_experts(value, kept_two, dense_two, True, [cot_rows])
    kept_two["low"] = value_low
    produced, grad_rows, *grads_two = run_experts_both(
        kept_two["received"], cot_rows, *experts_two
    )
    grad_sent = to_experts(grad_rows)
    sums_two = summed_shards(grads_two)
    grad_two, grads_of_two, _, grad_attn, (slot_rows,) = backward_from_experts(
        cot, grad_sent, None, dense_two, kept_two, kept_one["gates"]
    )
    out_two, _ = combined(tied(produced, grad_attn), kept_two)

    grad_out = grad_two.astype(LOW)
    grad_rows = to_experts(slot_rows)
    if relayed:
        early_parts, late_parts = dense_grads(*grads_of_two)
        grad_rows = tied(grad_rows, *late_parts, *early_parts)
        early_hop = first_hop(early_parts, 2, 1)
    grad_rows, out_two = lax.optimization_barrier((grad_rows, out_two))
    second_grads = run_experts_second(pre_one, grad_rows, experts_one[1])
    sums_one = summed_shards([second_grads])
    grad_rows, first_grads = run_experts_back(
        kept_one["received"], grad_rows, tied(pre_one, second_grads), *experts_one
    )
    sums_one = summed_shards([first_grads]) + sums_one
    activations = regrouped(jnp.where(is_first, out_one, out_two).reshape(held, rows, width))
    grad_sent = to_experts(grad_rows)
    late_two = []
    if relayed:
        grad_sent, early_hop = lax.optimization_barrier((grad_sent, early_hop))
        late_two = sent_along_exp([tied(one, grad_sent) for one in late_parts])
    grad_one, grads_of_one, grad_qkv, _, _ = backward_from_experts(
        grad_out, grad_sent, returned_one, dense_one, kept_one, None, late_two
    )
    came = [swapped(one) for one in chosen_by_core(words, sums_two, sums_one)]
    if relayed:
        late_parts_two = late_parts
        early_parts, late_parts = dense_grads(*grads_of_one)
        late_two = [tied(one, late_parts[0]) for one in late_two]
        late_one = sent_along_exp(late_parts)
        early_one = over_ctx(early_parts)
        early_hop = [tied(one, late_one[0]) for one in early_hop]
        early_two = finished_along_exp(last_hop(early_hop, 1))
        dense_sum_one = jnp.concatenate(
            [finished_along_exp(early_one), finished_along_ctx(late_parts, late_one)], axis=1
        )
        dense_sum_two = jnp.concatenate(
            [early_two, finished_along_ctx(late_parts_two, late_two)], axis=1
        )
    else:
        dense_sum_two = whole_dense_grads(*grads_of_two)
        dense_sum_one = whole_dense_grads(*grads_of_one)

    grads_in = regrouped(jnp.where(is_first, grad_one, grad_two).reshape(held, rows, width))
    dense_own = jnp.where(is_first, dense_sum_one, dense_sum_two)
    dense_came = swapped(jnp.where(is_first, dense_sum_two, dense_sum_one))
    dense_own, *came = lax.optimization_barrier((dense_own, *came))
    query_out, key_out, value_out, outproj_out, tail = unpack_dense(
        words, dense_own, dense_came, width
    )
    rel_out = tail[:, 2 + experts : 2 + experts + rel_cols].reshape(rel_bias.shape)
    first_out, second_out = join_experts(words, sums_one, sums_two, came)
    out_shape = (1, held, 1, rows, width)
    return (
        activations.reshape(out_shape),
        grads_in.reshape(out_shape),
        tail[:, 0][None],
        query_out[None],
        key_out[None],
        value_out[None],
        outproj_out[None],
        rel_out,
        tail[:, 1][None],
        tail[:, 2 : 2 + experts][None],
        first_out[None],
        second_out[None],
    )


def solution(mesh):
    rows_spec = P("section", ("ctx", "exp"), None)
    gain_spec = P("section", ("ctx", "exp"))
    expert_spec = P("section", "exp", "ctx", None)
    token_spec = P(None, "exp", "ctx", None)
    state_spec = P("section", None, "exp", "ctx", None)
    in_specs = (
        token_spec,
        token_spec,
        P(None, "exp", None),
        P(),
        token_spec,
        gain_spec,
        *[rows_spec] * 5,
        gain_spec,
        rows_spec,
        *[expert_spec] * 2,
    )
    out_specs = (
        *[state_spec] * 2,
        gain_spec,
        *[rows_spec] * 5,
        gain_spec,
        rows_spec,
        *[expert_spec] * 2,
    )
    return jax.shard_map(body, mesh=mesh, in_specs=in_specs, out_specs=out_specs, check_vma=False)
```
